32 devices in a mesh: dp: 8 (over z, x), mp: 4 (over y, core).
Axes of the slice: x: 2, y: 2, z: 4, core: 2. Of those that a mesh axis runs over, the one named last changes fastest.
Arguments:
- teacher_in: bfloat16 [512, 16384], P('dp', 'mp'), may hold values from -6 to 6
- teacher_weight: bfloat16 [16384, 8192], P('mp', 'dp'), may hold values from -0.046875 to 0.046875
- student_in: bfloat16 [512, 8192], P('dp', 'mp'), may hold values from -6 to 6
- projection: bfloat16 [8192, 8192], P('mp', 'dp'), may hold values from -0.0625 to 0.0625
- owner_order: int32 [512], P('mp'), may hold values from 0 to 127, as said below
Outputs:
- projection_grad: float32 [8192, 8192], P('mp', 'dp')
- cosine: float32 [512], P('mp')
The draws below stay inside these ranges and needn't reach their ends.
Inputs may be any that keep to these rules, and one draw needn't show every extreme that they name: `owner_order`: each aligned block of 128 entries is a permutation of 0 to 127.
All inputs are finite; a program needn't handle non-finite values.
Results may differ from the reference program's by a relative error of at most 0.025.
Values may be sent and summed in bfloat16 or wider, within the bound.
A program may use at most 64 MiB of HBM per device.

```python
import jax
import jax.numpy as jnp
from jax import lax

DT = 16384
DS = 8192
DTO = 8192
TOKENS = 512
N_MP = 4


def draw_owner_order(key, part):
    key = jax.random.fold_in(key, 7)
    block_keys = jax.random.split(key, N_MP)
    orders = jax.vmap(lambda single: jax.random.permutation(single, TOKENS // N_MP))(block_keys)
    return orders.reshape(-1).astype(jnp.int32)


def block_levels(own_key, dims, shards, smallest, high):
    level = 1.0
    for dim, parts in shards:
        heights = jax.random.uniform(jax.random.fold_in(jax.random.fold_in(own_key, 6), dim), (parts,), jnp.float32, smallest / len(shards), high / len(shards))
        level = level * jnp.repeat(jnp.exp(heights), dims[dim] // parts).reshape((-1,) + (1,) * (len(dims) - 1 - dim))
    return level


def gaussian(stream_key, dims, scale, bound, cuts=(), kind=jnp.bfloat16):
    values = jax.random.normal(stream_key, dims, jnp.float32) * scale
    if len(cuts) > 0:
        values = block_levels(stream_key, dims, cuts, -0.22, 0.18) * values
    return jnp.clip(values, min=-bound, max=bound).astype(kind)


def setup_inputs(seed: int = 0) -> dict:
    streams_of = jax.random.split(jax.random.key(seed), 6)
    teacher_in = gaussian(streams_of[0], (TOKENS, DT), 1.0, 6.0, ((0, 8), (1, 4)))
    teacher_weight = gaussian(streams_of[1], (DT, DTO), DT ** -0.5, 0.046875, ((0, 4), (1, 8)))
    student_in = gaussian(streams_of[2], (TOKENS, DS), 1.0, 6.0, ((0, 8), (1, 4)))
    projection = gaussian(streams_of[3], (DS, DTO), DS ** -0.5, 0.0625, ((0, 4), (1, 8)))
    owner_order = draw_owner_order(jax.random.fold_in(streams_of[5], 71), 0)
    return dict(teacher_in=teacher_in, teacher_weight=teacher_weight, student_in=student_in, projection=projection, owner_order=owner_order)


def block_sum(left, right, nblocks):
    width = left.shape[1] // nblocks

    def add_block(kk, running):
        left_cols = lax.dynamic_slice_in_dim(left, (kk * width).astype(jnp.int32), width, 1)
        right_rows = lax.dynamic_slice_in_dim(right, (kk * width).astype(jnp.int32), width, 0)
        product = jnp.dot(left_cols, right_rows, preferred_element_type=jnp.float32)
        rounded = lax.optimization_barrier(product.astype(jnp.bfloat16))
        return running + rounded.astype(jnp.float32)
    start_sum = jnp.zeros((left.shape[0], right.shape[1]), jnp.float32)
    return lax.fori_loop(jnp.int32(0), jnp.int32(nblocks), add_block, start_sum)

def reference(teacher_in, teacher_weight, student_in, projection, owner_order):
    block_len = TOKENS // N_MP
    sub_len = block_len // N_MP
    teacher_out = block_sum(teacher_in, teacher_weight, N_MP).astype(jnp.bfloat16)
    positions = jnp.arange(TOKENS, dtype=jnp.int32)
    owner = positions // block_len
    within = positions % block_len
    source_block = within // sub_len
    inner_pos = within % sub_len
    source = source_block * block_len + owner_order[source_block * block_len + owner * sub_len + inner_pos]
    target = teacher_out[source].astype(jnp.float32)
    student_out = block_sum(student_in, projection, N_MP)
    inner = lax.optimization_barrier(jnp.sum(student_out * target, axis=1))
    sq_student = lax.optimization_barrier(jnp.sum(student_out * student_out, axis=1))
    sq_target = lax.optimization_barrier(jnp.sum(target * target, axis=1))
    inv_student = lax.rsqrt(sq_student + 1e-06)
    inv_target = lax.rsqrt(sq_target + 1e-06)
    cosine = inner * inv_student * inv_target
    scale = -1.0 / TOKENS
    grad_out = scale * (target * (inv_student * inv_target)[:, None] - (inner * inv_target * inv_student ** 3)[:, None] * student_out)
    grad_out = grad_out.astype(jnp.bfloat16)
    projection_grad = lax.dot_general(student_in, grad_out, (((0,), (0,)), ((), ())), preferred_element_type=jnp.float32)
    return (projection_grad, cosine)
```

```python
import functools

import jax
import jax.numpy as jnp
from jax import lax
from jax.experimental import pallas as pl
from jax.experimental.pallas import tpu as pltpu
from jax.sharding import PartitionSpec as P

MESH = pl.DeviceIdType.MESH
F32 = jnp.float32
BF16 = jnp.bfloat16
TILE = 256


def kernel(
    total_rows,
    teacher_ref, weight_ref, student_ref, projection_ref, order_ref,
    cos_ref, dz_ref, st_ref,
    xbuf, wbuf, acc, stv, obuf, tsend, trecv, ssend, srecv, tf, zf, dzv, stm, statr,
    x_recv, send_a, send_b, send_x, local_x, local_w, o_send, o_recv,
    t_send, t_recv, s_send, s_recv, q_send, q_recv, d_send, d_recv, local_st, local_dz,
):
    dp, mp = lax.axis_index("dp"), lax.axis_index("mp")
    z, x = dp // 2, dp % 2
    ox = 1 - x
    za = z + 1 - 2 * (z % 2)
    zb = 3 - z
    half = z // 2
    mid = (z + 1) // 2 == 1
    order = [z, za, 2 - half, 3 - 3 * half]
    rows, width = xbuf.shape[3], xbuf.shape[4]
    block = 2 * rows
    sub = tsend.shape[2]
    cols = wbuf.shape[2]
    tiles = cols // TILE
    groups = 4

    def at(plane, column):
        return (2 * plane + column, mp)

    def mpd(other):
        return (dp, other)

    def other_mp(d):
        return (mp + d) % groups

    def own_src(t):
        if t < 2:
            return teacher_ref.at[:, pl.ds(t * width, width)]
        return student_ref

    w_copies = []
    x_copies = []
    for t in range(3):
        x_copies.append(pltpu.make_async_copy(own_src(t), xbuf.at[t, z, x], local_x.at[t]))
        src = weight_ref.at[pl.ds(t * width, width), :] if t < 2 else projection_ref
        w_copies.append(pltpu.make_async_copy(src, wbuf.at[t], local_w.at[t]))
    for t in range(3):
        x_copies[t].start()
        w_copies[t].start()

    barrier = pltpu.get_barrier_semaphore()
    for d in range(1, 8):
        pl.semaphore_signal(barrier, inc=1, device_id=((dp + d) % 8, mp), device_id_type=MESH)
    for d in range(1, groups):
        pl.semaphore_signal(barrier, inc=1, device_id=mpd(other_mp(d)), device_id_type=MESH)
    pl.semaphore_wait(barrier, 7 + groups - 1)

    def remote(src, dst, ssem, rsem, device):
        return pltpu.make_async_remote_copy(
            src_ref=src, dst_ref=dst, send_sem=ssem, recv_sem=rsem,
            device_id=device, device_id_type=MESH,
        )

    def copy_x(t, i):
        src = own_src(t) if i == 0 else xbuf.at[t, order[i], x]
        return remote(src, xbuf.at[t, order[i], x], send_x.at[t, i], x_recv.at[t, order[i], x], at(z, ox))

    def copy_a(t, i):
        if i == 1:
            src, s, c = xbuf.at[t, z, ox], z, ox
        else:
            s, c = order[i], x
            src = own_src(t) if i == 0 else xbuf.at[t, s, c]
        return remote(src, xbuf.at[t, s, c], send_a.at[t, i], x_recv.at[t, s, c], at(za, x))

    def copy_b(t, i):
        s = order[i]
        src = own_src(t) if i == 0 else xbuf.at[t, s, x]
        return remote(src, xbuf.at[t, s, x], send_b.at[t, i], x_recv.at[t, s, x], at(zb, x))

    def wait_piece(t, s, c):
        pltpu.make_async_copy(xbuf.at[t, s, c], xbuf.at[t, s, c], x_recv.at[t, s, c]).wait()

    def own(t):
        copy_a(t, 0).start()

        @pl.when(mid)
        def _():
            copy_b(t, 0).start()

        copy_x(t, 0).start()

    def event(t, i):
        wait_piece(t, order[i], x)

        @pl.when(mid)
        def _():
            (copy_b(t, 1) if i == 1 else copy_a(t, i)).start()

        if not (t == 2 and i == 1):
            copy_x(t, i).start()

    def other(t, i):
        wait_piece(t, order[i], ox)
        if t == 2 and i == 0:
            copy_a(t, 1).start()

    def lhs(t, s):
        return xbuf[t, s].reshape(block, width)

    def dot_tile(t, s, cs):
        return jnp.dot(lhs(t, s), wbuf[t, :, cs], preferred_element_type=F32)

    def tile_loop(body):
        def step(j, carry):
            body(pl.ds(pl.multiple_of(j * TILE, TILE), TILE))
            return carry

        lax.fori_loop(0, tiles, step, 0)

    def teacher_first(i):
        def body(cs):
            acc[i, :, cs] = dot_tile(0, order[i], cs)

        tile_loop(body)

    def teacher_second(i):
        b = order[i]

        def body(cs):
            part = (acc[i, :, cs] + dot_tile(1, b, cs)).astype(BF16)
            spread = lax.broadcasted_iota(jnp.int32, (block, block), 0) == jnp.broadcast_to(obuf[b], (block, block))
            picked = lax.dot_general(
                jnp.where(spread, 1.0, 0.0).astype(BF16), part, (((0,), (0,)), ((), ())), preferred_element_type=F32
            )
            tsend[b, :, :, cs] = picked.astype(BF16).reshape(groups, sub, TILE)

        tile_loop(body)
        for d in range(1, groups):
            o = other_mp(d)
            remote(tsend.at[b, o], trecv.at[mp, b], t_send.at[i, d], t_recv.at[mp, b], mpd(o)).start()

    def student_copy(b):
        return remote(ssend.at[b], srecv.at[mp], s_send.at[b], s_recv.at[mp], mpd(b))

    def student(i):
        b = order[i]

        def body(cs):
            ssend[b, :, cs] = dot_tile(2, b, cs).astype(BF16)

        tile_loop(body)

        @pl.when(mp != b)
        def _():
            student_copy(b).start()

    def st_copy(i):
        b = order[i]
        return pltpu.make_async_copy(
            stv.at[b], st_ref.at[:, pl.ds(pl.multiple_of(b * block, block), block)], local_st.at[i]
        )

    def transpose(i):
        b = order[i]

        def step(j, carry):
            ks = pl.ds(pl.multiple_of(j * TILE, TILE), TILE)
            stv[b, ks, :] = xbuf[2, b, :, :, ks].reshape(block, TILE).T
            return carry

        lax.fori_loop(0, width // TILE, step, 0)
        st_copy(i).start()

    obuf[mp] = order_ref[...]
    o_copies = [
        remote(order_ref, obuf.at[mp], o_send.at[d], o_recv.at[mp], mpd(other_mp(d))) for d in range(1, groups)
    ]

    own(0)
    for c in o_copies:
        c.start()
    own(1)
    event(0, 1)
    x_copies[0].wait()
    w_copies[0].wait()
    other(0, 0)
    teacher_first(0)
    event(0, 2)
    event(1, 1)
    event(0, 3)
    x_copies[1].wait()
    w_copies[1].wait()
    for d in range(1, groups):
        o = other_mp(d)
        pltpu.make_async_copy(obuf.at[o], obuf.at[o], o_recv.at[o]).wait()
    other(1, 0)
    teacher_second(0)
    other(0, 1)
    teacher_first(1)
    event(1, 2)
    own(2)
    other(0, 2)
    teacher_first(2)
    event(1, 3)
    other(0, 3)
    teacher_first(3)
    event(2, 1)
    other(1, 1)
    teacher_second(1)
    event(2, 2)
    other(1, 2)
    teacher_second(2)
    x_copies[2].wait()
    w_copies[2].wait()
    other(2, 0)
    student(0)
    transpose(0)
    event(2, 3)
    other(1, 3)
    teacher_second(3)
    other(2, 1)
    student(1)
    transpose(1)

    for d in range(1, groups):
        o = other_mp(d)
        for b in range(groups):
            pltpu.make_async_copy(trecv.at[o, b], trecv.at[o, b], t_recv.at[o, b]).wait()

    CH = 16
    per = sub // CH

    def target_step(r, carry):
        b, rs = r // per, pl.ds(pl.multiple_of((r % per) * CH, CH), CH)
        total = tsend[b, mp, rs, :].astype(F32)
        for d in range(1, groups):
            total = total + trecv[other_mp(d), b, rs, :].astype(F32)
        tf[pl.ds(pl.multiple_of(r * CH, CH), CH), :] = total.astype(BF16)
        return carry

    lax.fori_loop(0, block // CH, target_step, 0)

    other(2, 2)
    student(2)
    transpose(2)
    other(2, 3)
    student(3)
    transpose(3)

    for d in range(1, groups):
        o = other_mp(d)
        pltpu.make_async_copy(srecv.at[o], srecv.at[o], s_recv.at[o]).wait()

    def stats_step(r, carry):
        rs = pl.ds(pl.multiple_of(r * CH, CH), CH)
        zz = ssend[mp, rs, :].astype(F32)
        for d in range(1, groups):
            zz = zz + srecv[other_mp(d), rs, :].astype(F32)
        zf[rs, :] = zz
        tt = tf[rs, :].astype(F32)
        lane = lax.broadcasted_iota(jnp.int32, (CH, 128), 1)
        s0 = jnp.sum(zz * tt, axis=1, keepdims=True)
        s1 = jnp.sum(zz * zz, axis=1, keepdims=True)
        s2 = jnp.sum(tt * tt, axis=1, keepdims=True)
        stm[rs, :] = jnp.where(lane == 0, s0, jnp.where(lane == 1, s1, jnp.where(lane == 2, s2, 0.0)))
        return carry

    lax.fori_loop(0, block // CH, stats_step, 0)
    statr[dp] = stm[...].T[0:8, :]
    q_copies = []
    for d in range(1, 8):
        o = (dp + d) % 8
        q_copies.append(remote(statr.at[dp], statr.at[dp], q_send.at[d], q_recv.at[dp], (o, mp)))
    for c in q_copies:
        c.start()
    for d in range(1, 8):
        o = (dp + d) % 8
        pltpu.make_async_copy(statr.at[o], statr.at[o], q_recv.at[o]).wait()
    sums = statr[0]
    for s in range(1, 8):
        sums = sums + statr[s]
    inner = sums[0:1, :]
    inv_s = lax.rsqrt(sums[1:2, :] + 1e-06)
    inv_t = lax.rsqrt(sums[2:3, :] + 1e-06)
    cos_ref[...] = inner * inv_s * inv_t
    scale = -1.0 / total_rows
    on_target = jnp.broadcast_to(scale * (inv_s * inv_t), (block, block))
    on_student = jnp.broadcast_to(scale * (inner * inv_t * inv_s * inv_s * inv_s), (block, block))
    row = lax.broadcasted_iota(jnp.int32, (block, block), 0)
    stm[...] = jnp.where(row == 0, on_target, jnp.where(row == 1, on_student, 0.0)).T

    def dz_step(r, carry):
        rs = pl.ds(pl.multiple_of(r * CH, CH), CH)
        coef = stm[rs, :]
        dzv[rs, :] = (tf[rs, :].astype(F32) * coef[:, 0:1] - zf[rs, :] * coef[:, 1:2]).astype(BF16)
        return carry

    core = mp + 1 - 2 * (mp % 2)
    across = (mp + 2) % 4
    across_core = (core + 2) % 4

    def dz_at(o, h):
        return dz_ref.at[pl.ds(pl.multiple_of(o * block + h * rows, rows), rows), :]

    finals = []
    for h in range(2):
        lax.fori_loop(h * (rows // CH), (h + 1) * (rows // CH), dz_step, 0)
        src = dzv.at[pl.ds(h * rows, rows), :]
        far = remote(src, dz_at(mp, h), d_send.at[0, h], d_recv.at[mp, h], mpd(across))
        near = remote(src, dz_at(mp, h), d_send.at[1, h], d_recv.at[mp, h], mpd(core))
        mine = pltpu.make_async_copy(src, dz_at(mp, h), local_dz.at[h])
        far.start()
        near.start()
        mine.start()
        finals += [far, near]
    for h in range(2):
        pltpu.make_async_copy(dz_at(across, h), dz_at(across, h), d_recv.at[across, h]).wait()
        relay = remote(dz_at(across, h), dz_at(across, h), d_send.at[2, h], d_recv.at[across, h], mpd(core))
        relay.start()
        finals.append(relay)
    for h in range(2):
        for o in (core, across_core):
            pltpu.make_async_copy(dz_at(o, h), dz_at(o, h), d_recv.at[o, h]).wait()
        pltpu.make_async_copy(dzv.at[pl.ds(h * rows, rows), :], dz_at(mp, h), local_dz.at[h]).wait()

    for c in finals + q_copies + o_copies:
        c.wait_send()
    for t in range(3):
        copy_a(t, 0).wait_send()
        for i in range(groups):
            if not (t == 2 and i == 1):
                copy_x(t, i).wait_send()

        @pl.when(mid)
        def _():
            copy_b(t, 0).wait_send()
            copy_b(t, 1).wait_send()
            copy_a(t, 2).wait_send()
            copy_a(t, 3).wait_send()

    copy_a(2, 1).wait_send()
    for i in range(groups):
        b = order[i]
        for d in range(1, groups):
            o = other_mp(d)
            remote(tsend.at[b, o], trecv.at[mp, b], t_send.at[i, d], t_recv.at[mp, b], mpd(o)).wait_send()

        @pl.when(mp != b)
        def _():
            student_copy(b).wait_send()

        st_copy(i).wait()


def fused_shards(total_rows, teacher_in, teacher_weight, student_in, projection, owner_order):
    rows, width = student_in.shape
    cols = projection.shape[1]
    block = owner_order.shape[0]
    groups = total_rows // block
    sub = block // groups
    any_spec = pl.BlockSpec(memory_space=pl.ANY)
    vmem_spec = pl.BlockSpec(memory_space=pltpu.VMEM)
    dma = pltpu.SemaphoreType.DMA
    cos, dz, st = pl.pallas_call(
        functools.partial(kernel, total_rows),
        out_shape=(
            jax.ShapeDtypeStruct((1, block), F32),
            jax.ShapeDtypeStruct((total_rows, cols), BF16),
            jax.ShapeDtypeStruct((width, total_rows), BF16),
        ),
        in_specs=[any_spec] * 4 + [vmem_spec],
        out_specs=(vmem_spec, any_spec, any_spec),
        scratch_shapes=[
            pltpu.VMEM((3, 4, 2, rows, width), BF16),
            pltpu.VMEM((3, width, cols), BF16),
            pltpu.VMEM((4, block, cols), F32),
            pltpu.VMEM((4, width, block), BF16),
            pltpu.VMEM((4, 1, block), jnp.int32),
            pltpu.VMEM((4, groups, sub, cols), BF16),
            pltpu.VMEM((4, groups, sub, cols), BF16),
            pltpu.VMEM((4, block, cols), BF16),
            pltpu.VMEM((4, block, cols), BF16),
            pltpu.VMEM((block, cols), BF16),
            pltpu.VMEM((block, cols), F32),
            pltpu.VMEM((block, cols), BF16),
            pltpu.VMEM((block, 128), F32),
            pltpu.VMEM((8, 8, 128), F32),
            dma((3, 4, 2)),
            dma((3, 4)),
            dma((3, 2)),
            dma((3, 4)),
            dma((3,)),
            dma((3,)),
            dma((4,)),
            dma((4,)),
            dma((4, 4)),
            dma((4, 4)),
            dma((4,)),
            dma((4,)),
            dma((8,)),
            dma((8,)),
            dma((3, 2)),
            dma((4, 2)),
            dma((4,)),
            dma((2,)),
        ],
        compiler_params=pltpu.CompilerParams(
            collective_id=0, has_side_effects=True, vmem_limit_bytes=56 * 1024 * 1024
        ),
        name="distill",
    )(teacher_in, teacher_weight, student_in, projection, owner_order.reshape(1, block))
    grad = jnp.dot(st, dz, preferred_element_type=F32)
    return grad, cos.reshape(block)


def shards(teacher_in, teacher_weight, student_in, projection, owner_order):
    teacher_all = lax.all_gather(teacher_in, "dp", axis=0, tiled=True)
    student_all = lax.all_gather(student_in, "dp", axis=0, tiled=True)
    groups = lax.axis_size("mp")
    total_rows = teacher_all.shape[0]
    block_len = total_rows // groups
    sub_len = block_len // groups
    slab = teacher_all
    owned = lax.psum_scatter(
        jnp.dot(slab, teacher_weight, preferred_element_type=jnp.float32).astype(jnp.bfloat16),
        "mp",
        scatter_dimension=0,
        tiled=True,
    )
    picked = owned[owner_order].reshape(groups, sub_len, owned.shape[1])
    arrived = lax.all_to_all(picked, "mp", split_axis=0, concat_axis=0, tiled=True)
    target = arrived.reshape(block_len, owned.shape[1])
    slab = student_all
    student_out = lax.psum_scatter(
        jnp.dot(slab, projection, preferred_element_type=jnp.float32).astype(jnp.bfloat16),
        "mp",
        scatter_dimension=0,
        tiled=True,
    ).astype(jnp.float32)
    target_f = target.astype(jnp.float32)
    inner, sq_student, sq_target = lax.psum(
        (
            jnp.sum(student_out * target_f, axis=1),
            jnp.sum(student_out * student_out, axis=1),
            jnp.sum(target_f * target_f, axis=1),
        ),
        "dp",
    )
    inv_student = lax.rsqrt(sq_student + 1e-06)
    inv_target = lax.rsqrt(sq_target + 1e-06)
    cosine = inner * inv_student * inv_target
    scale = -1.0 / total_rows
    grad_out = scale * (
        target_f * (inv_student * inv_target)[:, None]
        - (inner * inv_target * inv_student**3)[:, None] * student_out
    )
    grad_out = grad_out.astype(jnp.bfloat16)
    projection_grad = lax.dot_general(
        student_all,
        lax.all_gather(grad_out, "mp", axis=0, tiled=True),
        (((0,), (0,)), ((), ())),
        preferred_element_type=jnp.float32,
    )
    return (projection_grad, cosine)


def solution(mesh):
    fits = mesh.shape["dp"] == 8 and mesh.shape["mp"] == 4

    def step(teacher_in, teacher_weight, student_in, projection, owner_order):
        args = (teacher_in, teacher_weight, student_in, projection, owner_order)
        if fits:
            return fused_shards(owner_order.shape[0] * mesh.shape["mp"], *args)
        return shards(*args)

    return jax.shard_map(
        step,
        mesh=mesh,
        in_specs=(P("dp", "mp"), P("mp", "dp"), P("dp", "mp"), P("mp", "dp"), P("mp")),
        out_specs=(P("mp", "dp"), P("mp")),
        check_vma=False,
    )
```

```python
import functools

import jax
import jax.numpy as jnp
from jax import lax
from jax.experimental import pallas as pl
from jax.experimental.pallas import tpu as pltpu
from jax.sharding import PartitionSpec as P

MESH = pl.DeviceIdType.MESH
F32 = jnp.float32
BF16 = jnp.bfloat16
TILE = 256


def kernel(
    total_rows,
    teacher_ref, weight_ref, student_ref, projection_ref, order_ref,
    cos_ref, dz_ref, st_ref,
    xbuf, wbuf, acc, stv, obuf, tsend, trecv, ssend, srecv, tall, zall, dzv, stm, statr, coef,
    x_recv, send_a, send_b, send_x, local_x, local_w, o_send, o_recv,
    t_send, t_recv, s_send, s_recv, q_send, q_recv, g_send, g_recv, z_send, z_recv, c_send, c_recv,
    local_st, local_dz,
):
    dp, mp = lax.axis_index("dp"), lax.axis_index("mp")
    z, x = dp // 2, dp % 2
    ox = 1 - x
    za = z + 1 - 2 * (z % 2)
    zb = 3 - z
    half = z // 2
    mid = (z + 1) // 2 == 1
    order = [z, za, 2 - half, 3 - 3 * half]
    rows, width = xbuf.shape[3], xbuf.shape[4]
    block = 2 * rows
    sub = tsend.shape[2]
    cols = wbuf.shape[2]
    tiles = cols // TILE
    groups = 4

    def at(plane, column):
        return (2 * plane + column, mp)

    def mpd(other):
        return (dp, other)

    def other_mp(d):
        return (mp + d) % groups

    def own_src(t):
        if t > 0:
            return teacher_ref.at[:, pl.ds((t - 1) * width, width)]
        return student_ref

    w_copies = []
    x_copies = []
    for t in range(3):
        x_copies.append(pltpu.make_async_copy(own_src(t), xbuf.at[t, z, x], local_x.at[t]))
        src = weight_ref.at[pl.ds((t - 1) * width, width), :] if t > 0 else projection_ref
        w_copies.append(pltpu.make_async_copy(src, wbuf.at[t], local_w.at[t]))
    for t in range(3):
        x_copies[t].start()
        w_copies[t].start()

    barrier = pltpu.get_barrier_semaphore()
    for d in range(1, 8):
        pl.semaphore_signal(barrier, inc=1, device_id=((dp + d) % 8, mp), device_id_type=MESH)
    for d in range(1, groups):
        pl.semaphore_signal(barrier, inc=1, device_id=mpd(other_mp(d)), device_id_type=MESH)
    pl.semaphore_wait(barrier, 7 + groups - 1)

    def remote(src, dst, ssem, rsem, device):
        return pltpu.make_async_remote_copy(
            src_ref=src, dst_ref=dst, send_sem=ssem, recv_sem=rsem,
            device_id=device, device_id_type=MESH,
        )

    def copy_x(t, i):
        src = own_src(t) if i == 0 else xbuf.at[t, order[i], x]
        return remote(src, xbuf.at[t, order[i], x], send_x.at[t, i], x_recv.at[t, order[i], x], at(z, ox))

    def copy_a(t, i):
        if i == 1:
            src, s, c = xbuf.at[t, z, ox], z, ox
        else:
            s, c = order[i], x
            src = own_src(t) if i == 0 else xbuf.at[t, s, c]
        return remote(src, xbuf.at[t, s, c], send_a.at[t, i], x_recv.at[t, s, c], at(za, x))

    def copy_b(t, i):
        s = order[i]
        src = own_src(t) if i == 0 else xbuf.at[t, s, x]
        return remote(src, xbuf.at[t, s, x], send_b.at[t, i], x_recv.at[t, s, x], at(zb, x))

    def wait_piece(t, s, c):
        pltpu.make_async_copy(xbuf.at[t, s, c], xbuf.at[t, s, c], x_recv.at[t, s, c]).wait()

    def own(t):
        copy_a(t, 0).start()

        @pl.when(mid)
        def _():
            copy_b(t, 0).start()

        copy_x(t, 0).start()

    def event(t, i):
        wait_piece(t, order[i], x)

        @pl.when(mid)
        def _():
            (copy_b(t, 1) if i == 1 else copy_a(t, i)).start()

        if not (t == 2 and i == 1):
            copy_x(t, i).start()

    def other(t, i):
        wait_piece(t, order[i], ox)
        if t == 2 and i == 0:
            copy_a(t, 1).start()

    def lhs(t, s):
        return xbuf[t, s].reshape(block, width)

    def dot_tile(t, s, cs):
        return jnp.dot(lhs(t, s), wbuf[t, :, cs], preferred_element_type=F32)

    def tile_loop(body):
        def step(j, carry):
            body(pl.ds(pl.multiple_of(j * TILE, TILE), TILE))
            return carry

        lax.fori_loop(0, tiles, step, 0)

    def teacher_first(i):
        def body(cs):
            acc[i, :, cs] = dot_tile(1, order[i], cs)

        tile_loop(body)

    def teacher_second(i):
        b = order[i]

        def body(cs):
            part = (acc[i, :, cs] + dot_tile(2, b, cs)).astype(BF16)
            spread = lax.broadcasted_iota(jnp.int32, (block, block), 0) == jnp.broadcast_to(obuf[b], (block, block))
            picked = lax.dot_general(
                jnp.where(spread, 1.0, 0.0).astype(BF16), part, (((0,), (0,)), ((), ())), preferred_element_type=F32
            )
            tsend[b, :, :, cs] = picked.astype(BF16).reshape(groups, sub, TILE)

        tile_loop(body)
        for d in range(1, groups):
            o = other_mp(d)
            remote(tsend.at[b, o], trecv.at[mp, b], t_send.at[i, d], t_recv.at[mp, b], mpd(o)).start()

    def student_copy(b):
        return remote(ssend.at[b], srecv.at[mp], s_send.at[b], s_recv.at[mp], mpd(b))

    def student(i):
        b = order[i]

        def body(cs):
            ssend[b, :, cs] = dot_tile(0, b, cs).astype(BF16)

        tile_loop(body)

        @pl.when(mp != b)
        def _():
            student_copy(b).start()

    def st_copy(i):
        b = order[i]
        return pltpu.make_async_copy(
            stv.at[b], st_ref.at[:, pl.ds(pl.multiple_of(b * block, block), block)], local_st.at[i]
        )

    def transpose(i):
        b = order[i]

        def step(j, carry):
            ks = pl.ds(pl.multiple_of(j * TILE, TILE), TILE)
            stv[b, ks, :] = xbuf[0, b, :, :, ks].reshape(block, TILE).T
            return carry

        lax.fori_loop(0, width // TILE, step, 0)
        st_copy(i).start()

    obuf[mp] = order_ref[...]
    o_copies = [
        remote(order_ref, obuf.at[mp], o_send.at[d], o_recv.at[mp], mpd(other_mp(d))) for d in range(1, groups)
    ]

    CH = 16
    core = mp + 1 - 2 * (mp % 2)
    across = (mp + 2) % 4
    across_core = (core + 2) % 4

    def arrived(ref, sem):
        pltpu.make_async_copy(ref, ref, sem).wait()

    def z_copy(k):
        o, to = ((mp, across), (mp, core), (across, core))[k]
        return remote(zall.at[o], zall.at[o], z_send.at[k], z_recv.at[o], mpd(to))

    def student_sum():
        for d in range(1, groups):
            o = other_mp(d)
            arrived(srecv.at[o], s_recv.at[o])

        def step(r, carry):
            rs = pl.ds(pl.multiple_of(r * CH, CH), CH)
            total = ssend[mp, rs, :].astype(F32)
            for d in range(1, groups):
                total = total + srecv[other_mp(d), rs, :].astype(F32)
            zall[mp, rs, :] = total
            return carry

        lax.fori_loop(0, block // CH, step, 0)
        z_copy(0).start()
        z_copy(1).start()

    def student_relay():
        arrived(zall.at[across], z_recv.at[across])
        z_copy(2).start()

    def g_copy(i, k):
        b = order[i]
        o, to = ((mp, across), (mp, core), (across, core))[k]
        return remote(tall.at[o, b], tall.at[o, b], g_send.at[i, k], g_recv.at[o, b], mpd(to))

    def target_sum(i):
        b = order[i]
        for d in range(1, groups):
            o = other_mp(d)
            arrived(trecv.at[o, b], t_recv.at[o, b])
        for r in range(sub // CH):
            rs = pl.ds(r * CH, CH)
            total = tsend[b, mp, rs, :].astype(F32)
            for d in range(1, groups):
                total = total + trecv[other_mp(d), b, rs, :].astype(F32)
            tall[mp, b, rs, :] = total.astype(BF16)
        g_copy(i, 0).start()
        g_copy(i, 1).start()
        for r in range(sub // CH):
            rows_here = pl.ds(pl.multiple_of(b * sub + r * CH, CH), CH)
            tt = tall[mp, b, pl.ds(r * CH, CH), :].astype(F32)
            zz = zall[mp, rows_here, :]
            lane = lax.broadcasted_iota(jnp.int32, (CH, 128), 1)
            s0 = jnp.sum(zz * tt, axis=1, keepdims=True)
            s1 = jnp.sum(zz * zz, axis=1, keepdims=True)
            s2 = jnp.sum(tt * tt, axis=1, keepdims=True)
            stm[rows_here, :] = jnp.where(lane == 0, s0, jnp.where(lane == 1, s1, jnp.where(lane == 2, s2, 0.0)))

    def target_relay(i):
        b = order[i]
        arrived(tall.at[across, b], g_recv.at[across, b])
        g_copy(i, 2).start()

    own(0)
    for c in o_copies:
        c.start()
    own(1)
    event(0, 1)
    x_copies[0].wait()
    w_copies[0].wait()
    other(0, 0)
    student(0)
    event(0, 2)
    event(1, 1)
    event(0, 3)
    x_copies[1].wait()
    w_copies[1].wait()
    other(1, 0)
    teacher_first(0)
    other(0, 1)
    student(1)
    event(1, 2)
    own(2)
    other(0, 2)
    student(2)
    event(1, 3)
    other(0, 3)
    student(3)
    event(2, 1)
    other(1, 1)
    teacher_first(1)
    event(2, 2)
    student_sum()
    other(1, 2)
    teacher_first(2)
    x_copies[2].wait()
    w_copies[2].wait()
    for d in range(1, groups):
        o = other_mp(d)
        arrived(obuf.at[o], o_recv.at[o])
    other(2, 0)
    teacher_second(0)
    event(2, 3)
    student_relay()
    transpose(0)
    transpose(1)
    other(1, 3)
    teacher_first(3)
    transpose(2)
    transpose(3)
    other(2, 1)
    teacher_second(1)
    target_sum(0)
    other(2, 2)
    teacher_second(2)
    target_sum(1)
    target_relay(0)
    other(2, 3)
    teacher_second(3)
    target_sum(2)
    target_relay(1)
    target_sum(3)

    statr[dp] = stm[...].T[0:8, :]
    q_copies = []
    for d in range(1, 8):
        o = (dp + d) % 8
        q_copies.append(remote(statr.at[dp], statr.at[dp], q_send.at[d], q_recv.at[dp], (o, mp)))
    for c in q_copies:
        c.start()
    target_relay(2)
    target_relay(3)
    for d in range(1, 8):
        o = (dp + d) % 8
        arrived(statr.at[o], q_recv.at[o])
    sums = statr[0]
    for s in range(1, 8):
        sums = sums + statr[s]
    inner = sums[0:1, :]
    inv_s = lax.rsqrt(sums[1:2, :] + 1e-06)
    inv_t = lax.rsqrt(sums[2:3, :] + 1e-06)
    cos_ref[...] = inner * inv_s * inv_t
    scale = -1.0 / total_rows
    on_target = jnp.broadcast_to(scale * (inv_s * inv_t), (8, block))
    on_student = jnp.broadcast_to(scale * (inner * inv_t * inv_s * inv_s * inv_s), (8, block))
    row = lax.broadcasted_iota(jnp.int32, (8, block), 0)
    coef[mp] = jnp.where(row == 0, on_target, jnp.where(row == 1, on_student, 0.0))
    c_copies = [
        remote(coef.at[mp], coef.at[mp], c_send.at[d], c_recv.at[mp], mpd(other_mp(d))) for d in range(1, groups)
    ]
    for c in c_copies:
        c.start()

    def dz_copy(k, o):
        here = pl.ds(pl.multiple_of(o * block, block), block)
        return pltpu.make_async_copy(dzv.at[o], dz_ref.at[here, :], local_dz.at[k])

    owners = (mp, core, across, across_core)
    for k, o in enumerate(owners):
        if k > 0:
            arrived(coef.at[o], c_recv.at[o])
            if k != 2:
                for b in range(4):
                    arrived(tall.at[o, b], g_recv.at[o, b])
                arrived(zall.at[o], z_recv.at[o])
        stm[...] = jnp.concatenate([coef[o], jnp.zeros((block - 8, block), F32)], axis=0).T

        def dz_step(r, carry):
            rs = pl.ds(pl.multiple_of(r * CH, CH), CH)
            b, part = r * CH // sub, pl.ds(pl.multiple_of(r * CH % sub, CH), CH)
            both = stm[rs, :]
            dzv[o, rs, :] = (tall[o, b, part, :].astype(F32) * both[:, 0:1] - zall[o, rs, :] * both[:, 1:2]).astype(BF16)
            return carry

        lax.fori_loop(0, block // CH, dz_step, 0)
        dz_copy(k, o).start()

    for c in c_copies + q_copies + o_copies + [z_copy(k) for k in range(3)]:
        c.wait_send()
    for t in range(3):
        copy_a(t, 0).wait_send()
        for i in range(groups):
            if not (t == 2 and i == 1):
                copy_x(t, i).wait_send()

        @pl.when(mid)
        def _():
            copy_b(t, 0).wait_send()
            copy_b(t, 1).wait_send()
            copy_a(t, 2).wait_send()
            copy_a(t, 3).wait_send()

    copy_a(2, 1).wait_send()
    for i in range(groups):
        b = order[i]
        for d in range(1, groups):
            o = other_mp(d)
            remote(tsend.at[b, o], trecv.at[mp, b], t_send.at[i, d], t_recv.at[mp, b], mpd(o)).wait_send()
        for k in range(3):
            g_copy(i, k).wait_send()

        @pl.when(mp != b)
        def _():
            student_copy(b).wait_send()

        st_copy(i).wait()
        dz_copy(i, owners[i]).wait()


def grad_kernel(st_ref, dz_ref, out_ref):
    out_ref[...] = jnp.dot(st_ref[...], dz_ref[...], preferred_element_type=F32)


def grad_matmul(st, dz):
    width, depth = st.shape
    cols = dz.shape[1]
    return pl.pallas_call(
        grad_kernel,
        grid=(width // TILE,),
        in_specs=[
            pl.BlockSpec((TILE, depth), lambda i: (i, 0)),
            pl.BlockSpec((depth, cols), lambda i: (0, 0)),
        ],
        out_specs=pl.BlockSpec((TILE, cols), lambda i: (i, 0)),
        out_shape=jax.ShapeDtypeStruct((width, cols), F32),
        compiler_params=pltpu.CompilerParams(vmem_limit_bytes=32 * 1024 * 1024),
        name="grad",
    )(st, dz)


def fused_shards(total_rows, teacher_in, teacher_weight, student_in, projection, owner_order):
    rows, width = student_in.shape
    cols = projection.shape[1]
    block = owner_order.shape[0]
    groups = total_rows // block
    sub = block // groups
    any_spec = pl.BlockSpec(memory_space=pl.ANY)
    vmem_spec = pl.BlockSpec(memory_space=pltpu.VMEM)
    dma = pltpu.SemaphoreType.DMA
    cos, dz, st = pl.pallas_call(
        functools.partial(kernel, total_rows),
        out_shape=(
            jax.ShapeDtypeStruct((1, block), F32),
            jax.ShapeDtypeStruct((total_rows, cols), BF16),
            jax.ShapeDtypeStruct((width, total_rows), BF16),
        ),
        in_specs=[any_spec] * 4 + [vmem_spec],
        out_specs=(vmem_spec, any_spec, any_spec),
        scratch_shapes=[
            pltpu.VMEM((3, 4, 2, rows, width), BF16),
            pltpu.VMEM((3, width, cols), BF16),
            pltpu.VMEM((4, block, cols), F32),
            pltpu.VMEM((4, width, block), BF16),
            pltpu.VMEM((4, 1, block), jnp.int32),
            pltpu.VMEM((4, groups, sub, cols), BF16),
            pltpu.VMEM((4, groups, sub, cols), BF16),
            pltpu.VMEM((4, block, cols), BF16),
            pltpu.VMEM((4, block, cols), BF16),
            pltpu.VMEM((4, groups, sub, cols), BF16),
            pltpu.VMEM((4, block, cols), F32),
            pltpu.VMEM((4, block, cols), BF16),
            pltpu.VMEM((block, 128), F32),
            pltpu.VMEM((8, 8, 128), F32),
            pltpu.VMEM((4, 8, block), F32),
            dma((3, 4, 2)),
            dma((3, 4)),
            dma((3, 2)),
            dma((3, 4)),
            dma((3,)),
            dma((3,)),
            dma((4,)),
            dma((4,)),
            dma((4, 4)),
            dma((4, 4)),
            dma((4,)),
            dma((4,)),
            dma((8,)),
            dma((8,)),
            dma((4, 3)),
            dma((4, 4)),
            dma((3,)),
            dma((4,)),
            dma((4,)),
            dma((4,)),
            dma((4,)),
            dma((4,)),
        ],
        compiler_params=pltpu.CompilerParams(
            collective_id=0, has_side_effects=True, vmem_limit_bytes=56 * 1024 * 1024
        ),
        name="distill",
    )(teacher_in, teacher_weight, student_in, projection, owner_order.reshape(1, block))
    return grad_matmul(st, dz), cos.reshape(block)


def shards(teacher_in, teacher_weight, student_in, projection, owner_order):
    teacher_all = lax.all_gather(teacher_in, "dp", axis=0, tiled=True)
    student_all = lax.all_gather(student_in, "dp", axis=0, tiled=True)
    groups = lax.axis_size("mp")
    total_rows = teacher_all.shape[0]
    block_len = total_rows // groups
    sub_len = block_len // groups
    slab = teacher_all
    owned = lax.psum_scatter(
        jnp.dot(slab, teacher_weight, preferred_element_type=jnp.float32).astype(jnp.bfloat16),
        "mp",
        scatter_dimension=0,
        tiled=True,
    )
    picked = owned[owner_order].reshape(groups, sub_len, owned.shape[1])
    arrived = lax.all_to_all(picked, "mp", split_axis=0, concat_axis=0, tiled=True)
    target = arrived.reshape(block_len, owned.shape[1])
    slab = student_all
    student_out = lax.psum_scatter(
        jnp.dot(slab, projection, preferred_element_type=jnp.float32).astype(jnp.bfloat16),
        "mp",
        scatter_dimension=0,
        tiled=True,
    ).astype(jnp.float32)
    target_f = target.astype(jnp.float32)
    inner, sq_student, sq_target = lax.psum(
        (
            jnp.sum(student_out * target_f, axis=1),
            jnp.sum(student_out * student_out, axis=1),
            jnp.sum(target_f * target_f, axis=1),
        ),
        "dp",
    )
    inv_student = lax.rsqrt(sq_student + 1e-06)
    inv_target = lax.rsqrt(sq_target + 1e-06)
    cosine = inner * inv_student * inv_target
    scale = -1.0 / total_rows
    grad_out = scale * (
        target_f * (inv_student * inv_target)[:, None]
        - (inner * inv_target * inv_student**3)[:, None] * student_out
    )
    grad_out = grad_out.astype(jnp.bfloat16)
    projection_grad = lax.dot_general(
        student_all,
        lax.all_gather(grad_out, "mp", axis=0, tiled=True),
        (((0,), (0,)), ((), ())),
        preferred_element_type=jnp.float32,
    )
    return (projection_grad, cosine)


def solution(mesh):
    fits = mesh.shape["dp"] == 8 and mesh.shape["mp"] == 4

    def step(teacher_in, teacher_weight, student_in, projection, owner_order):
        args = (teacher_in, teacher_weight, student_in, projection, owner_order)
        if fits:
            return fused_shards(owner_order.shape[0] * mesh.shape["mp"], *args)
        return shards(*args)

    return jax.shard_map(
        step,
        mesh=mesh,
        in_specs=(P("dp", "mp"), P("mp", "dp"), P("dp", "mp"), P("mp", "dp"), P("mp")),
        out_specs=(P("mp", "dp"), P("mp")),
        check_vma=False,
    )
```

```python
import functools

import jax
import jax.numpy as jnp
from jax import lax
from jax.experimental import pallas as pl
from jax.experimental.pallas import tpu as pltpu
from jax.sharding import PartitionSpec as P

MESH = pl.DeviceIdType.MESH
F32 = jnp.float32
BF16 = jnp.bfloat16
TILE = 256


def kernel(
    total_rows,
    teacher_ref, weight_ref, student_ref, projection_ref, order_ref,
    cos_ref, dz_ref, st_ref,
    xbuf, wbuf, acc, stv, obuf, tsend, trecv, ssend, srecv, tall, zall, dzv, stm, statr, coef,
    x_recv, send_a, send_b, send_x, local_x, local_w, o_send, o_recv,
    t_send, t_recv, s_send, s_recv, q_send, q_recv, g_send, g_recv, z_send, z_recv, c_send, c_recv,
    local_st, local_dz,
):
    dp, mp = lax.axis_index("dp"), lax.axis_index("mp")
    z, x = dp // 2, dp % 2
    ox = 1 - x
    za = z + 1 - 2 * (z % 2)
    zb = 3 - z
    half = z // 2
    mid = (z + 1) // 2 == 1
    order = [z, za, 2 - half, 3 - 3 * half]
    rows, width = xbuf.shape[3], xbuf.shape[4]
    block = 2 * rows
    sub = tsend.shape[2]
    cols = wbuf.shape[2]
    tiles = cols // TILE
    groups = 4

    def at(plane, column):
        return (2 * plane + column, mp)

    def mpd(other):
        return (dp, other)

    def other_mp(d):
        return (mp + d) % groups

    def own_src(t):
        if t > 0:
            return teacher_ref.at[:, pl.ds((t - 1) * width, width)]
        return student_ref

    w_copies = []
    x_copies = []
    for t in range(3):
        x_copies.append(pltpu.make_async_copy(own_src(t), xbuf.at[t, z, x], local_x.at[t]))
        src = weight_ref.at[pl.ds((t - 1) * width, width), :] if t > 0 else projection_ref
        w_copies.append(pltpu.make_async_copy(src, wbuf.at[t], local_w.at[t]))
    for t in range(3):
        x_copies[t].start()
        w_copies[t].start()

    barrier = pltpu.get_barrier_semaphore()
    for d in range(1, 8):
        pl.semaphore_signal(barrier, inc=1, device_id=((dp + d) % 8, mp), device_id_type=MESH)
    for d in range(1, groups):
        pl.semaphore_signal(barrier, inc=1, device_id=mpd(other_mp(d)), device_id_type=MESH)
    pl.semaphore_wait(barrier, 7 + groups - 1)

    def remote(src, dst, ssem, rsem, device):
        return pltpu.make_async_remote_copy(
            src_ref=src, dst_ref=dst, send_sem=ssem, recv_sem=rsem,
            device_id=device, device_id_type=MESH,
        )

    def copy_x(t, i):
        src = own_src(t) if i == 0 else xbuf.at[t, order[i], x]
        return remote(src, xbuf.at[t, order[i], x], send_x.at[t, i], x_recv.at[t, order[i], x], at(z, ox))

    def copy_a(t, i):
        if i == 1:
            src, s, c = xbuf.at[t, z, ox], z, ox
        else:
            s, c = order[i], x
            src = own_src(t) if i == 0 else xbuf.at[t, s, c]
        return remote(src, xbuf.at[t, s, c], send_a.at[t, i], x_recv.at[t, s, c], at(za, x))

    def copy_b(t, i):
        s = order[i]
        src = own_src(t) if i == 0 else xbuf.at[t, s, x]
        return remote(src, xbuf.at[t, s, x], send_b.at[t, i], x_recv.at[t, s, x], at(zb, x))

    def wait_piece(t, s, c):
        pltpu.make_async_copy(xbuf.at[t, s, c], xbuf.at[t, s, c], x_recv.at[t, s, c]).wait()

    def own(t):
        copy_a(t, 0).start()

        @pl.when(mid)
        def _():
            copy_b(t, 0).start()

        copy_x(t, 0).start()

    def event(t, i):
        wait_piece(t, order[i], x)

        @pl.when(mid)
        def _():
            (copy_b(t, 1) if i == 1 else copy_a(t, i)).start()

        if not (t == 2 and i == 1):
            copy_x(t, i).start()

    def other(t, i):
        wait_piece(t, order[i], ox)
        if t == 2 and i == 0:
            copy_a(t, 1).start()

    bases = [2 * half, 2 - 2 * half]

    def dot_pair(t, p, cs):
        left = xbuf[t, pl.ds(bases[p], 2)].reshape(2 * block, width)
        return jnp.dot(left, wbuf[t, :, cs], preferred_element_type=F32)

    def tile_loop(body):
        def step(j, carry):
            body(pl.ds(pl.multiple_of(j * TILE, TILE), TILE))
            return carry

        lax.fori_loop(0, tiles, step, 0)

    def spread(b):
        hit = lax.broadcasted_iota(jnp.int32, (block, block), 0) == jnp.broadcast_to(obuf[b], (block, block))
        return jnp.where(hit, 1.0, 0.0).astype(BF16)

    def permute(b, part, cs):
        picked = lax.dot_general(spread(b), part, (((0,), (0,)), ((), ())), preferred_element_type=F32)
        tsend[b, :, :, cs] = picked.astype(BF16).reshape(groups, sub, TILE)

    def teacher_send(i):
        b = order[i]
        for d in range(1, groups):
            o = other_mp(d)
            remote(tsend.at[b, o], trecv.at[mp, b], t_send.at[i, d], t_recv.at[mp, b], mpd(o)).start()

    def teacher_first(p):
        def body(cs):
            acc[pl.ds(bases[p], 2), :, cs] = dot_pair(1, p, cs).reshape(2, block, TILE)

        tile_loop(body)

    def teacher_pair():
        b = bases[0]

        def body(cs):
            part = (acc[pl.ds(b, 2), :, cs].reshape(2 * block, TILE) + dot_pair(2, 0, cs)).astype(BF16)
            permute(b, part[:block], cs)
            permute(b + 1, part[block:], cs)

        tile_loop(body)
        teacher_send(0)
        teacher_send(1)

    def teacher_second(i):
        b = order[i]

        def body(cs):
            new = jnp.dot(xbuf[2, b].reshape(block, width), wbuf[2, :, cs], preferred_element_type=F32)
            permute(b, (acc[b, :, cs] + new).astype(BF16), cs)

        tile_loop(body)
        teacher_send(i)

    def student_copy(b):
        return remote(ssend.at[b], srecv.at[mp], s_send.at[b], s_recv.at[mp], mpd(b))

    def student(p):
        def body(cs):
            ssend[pl.ds(bases[p], 2), :, cs] = dot_pair(0, p, cs).astype(BF16).reshape(2, block, TILE)

        tile_loop(body)
        for i in (2 * p, 2 * p + 1):
            b = order[i]

            @pl.when(mp != b)
            def _():
                student_copy(b).start()

    def st_copy(i):
        b = order[i]
        return pltpu.make_async_copy(
            stv.at[b], st_ref.at[:, pl.ds(pl.multiple_of(b * block, block), block)], local_st.at[i]
        )

    def transpose(i):
        b = order[i]

        def step(j, carry):
            ks = pl.ds(pl.multiple_of(j * TILE, TILE), TILE)
            stv[b, ks, :] = xbuf[0, b, :, :, ks].reshape(block, TILE).T
            return carry

        lax.fori_loop(0, width // TILE, step, 0)
        st_copy(i).start()

    obuf[mp] = order_ref[...]
    o_copies = [
        remote(order_ref, obuf.at[mp], o_send.at[d], o_recv.at[mp], mpd(other_mp(d))) for d in range(1, groups)
    ]

    CH = 16
    core = mp + 1 - 2 * (mp % 2)
    across = (mp + 2) % 4
    across_core = (core + 2) % 4

    def arrived(ref, sem):
        pltpu.make_async_copy(ref, ref, sem).wait()

    def z_copy(k):
        o, to = ((mp, across), (mp, core), (across, core))[k]
        return remote(zall.at[o], zall.at[o], z_send.at[k], z_recv.at[o], mpd(to))

    def student_sum():
        for d in range(1, groups):
            o = other_mp(d)
            arrived(srecv.at[o], s_recv.at[o])

        def step(r, carry):
            rs = pl.ds(pl.multiple_of(r * CH, CH), CH)
            total = ssend[mp, rs, :].astype(F32)
            for d in range(1, groups):
                total = total + srecv[other_mp(d), rs, :].astype(F32)
            zall[mp, rs, :] = total
            return carry

        lax.fori_loop(0, block // CH, step, 0)
        z_copy(0).start()
        z_copy(1).start()

    def student_relay():
        arrived(zall.at[across], z_recv.at[across])
        z_copy(2).start()

    def g_copy(i, k):
        b = order[i]
        o, to = ((mp, across), (mp, core), (across, core))[k]
        return remote(tall.at[o, b], tall.at[o, b], g_send.at[i, k], g_recv.at[o, b], mpd(to))

    def target_sum(i):
        b = order[i]
        for d in range(1, groups):
            o = other_mp(d)
            arrived(trecv.at[o, b], t_recv.at[o, b])
        for r in range(sub // CH):
            rs = pl.ds(r * CH, CH)
            total = tsend[b, mp, rs, :].astype(F32)
            for d in range(1, groups):
                total = total + trecv[other_mp(d), b, rs, :].astype(F32)
            tall[mp, b, rs, :] = total.astype(BF16)
        g_copy(i, 0).start()
        g_copy(i, 1).start()
        for r in range(sub // CH):
            rows_here = pl.ds(pl.multiple_of(b * sub + r * CH, CH), CH)
            tt = tall[mp, b, pl.ds(r * CH, CH), :].astype(F32)
            zz = zall[mp, rows_here, :]
            lane = lax.broadcasted_iota(jnp.int32, (CH, 128), 1)
            s0 = jnp.sum(zz * tt, axis=1, keepdims=True)
            s1 = jnp.sum(zz * zz, axis=1, keepdims=True)
            s2 = jnp.sum(tt * tt, axis=1, keepdims=True)
            stm[rows_here, :] = jnp.where(lane == 0, s0, jnp.where(lane == 1, s1, jnp.where(lane == 2, s2, 0.0)))

    def target_relay(i):
        b = order[i]
        arrived(tall.at[across, b], g_recv.at[across, b])
        g_copy(i, 2).start()

    own(0)
    for c in o_copies:
        c.start()
    own(1)
    event(0, 1)
    event(1, 1)
    event(0, 2)
    other(0, 0)
    event(0, 3)
    x_copies[0].wait()
    w_copies[0].wait()
    other(0, 1)
    student(0)
    event(1, 2)
    own(2)
    x_copies[1].wait()
    w_copies[1].wait()
    other(1, 0)
    other(1, 1)
    teacher_first(0)
    event(1, 3)
    other(0, 2)
    other(0, 3)
    student(1)
    event(2, 1)
    transpose(0)
    transpose(1)
    other(2, 0)
    event(2, 2)
    student_sum()
    transpose(2)
    transpose(3)
    event(2, 3)
    other(1, 2)
    other(1, 3)
    teacher_first(1)
    student_relay()
    x_copies[2].wait()
    w_copies[2].wait()
    for d in range(1, groups):
        o = other_mp(d)
        arrived(obuf.at[o], o_recv.at[o])
    other(2, 1)
    teacher_pair()
    target_sum(0)
    target_sum(1)
    other(2, 2)
    teacher_second(2)
    target_relay(0)
    target_relay(1)
    other(2, 3)
    teacher_second(3)
    target_sum(2)
    target_sum(3)

    statr[dp] = stm[...].T[0:8, :]
    q_copies = []
    for d in range(1, 8):
        o = (dp + d) % 8
        q_copies.append(remote(statr.at[dp], statr.at[dp], q_send.at[d], q_recv.at[dp], (o, mp)))
    for c in q_copies:
        c.start()
    target_relay(2)
    target_relay(3)
    for d in range(1, 8):
        o = (dp + d) % 8
        arrived(statr.at[o], q_recv.at[o])
    sums = statr[0]
    for s in range(1, 8):
        sums = sums + statr[s]
    inner = sums[0:1, :]
    inv_s = lax.rsqrt(sums[1:2, :] + 1e-06)
    inv_t = lax.rsqrt(sums[2:3, :] + 1e-06)
    cos_ref[...] = inner * inv_s * inv_t
    scale = -1.0 / total_rows
    on_target = jnp.broadcast_to(scale * (inv_s * inv_t), (8, block))
    on_student = jnp.broadcast_to(scale * (inner * inv_t * inv_s * inv_s * inv_s), (8, block))
    row = lax.broadcasted_iota(jnp.int32, (8, block), 0)
    coef[mp] = jnp.where(row == 0, on_target, jnp.where(row == 1, on_student, 0.0))
    c_copies = [
        remote(coef.at[mp], coef.at[mp], c_send.at[d], c_recv.at[mp], mpd(other_mp(d))) for d in range(1, groups)
    ]
    for c in c_copies:
        c.start()

    def dz_copy(k, o):
        here = pl.ds(pl.multiple_of(o * block, block), block)
        return pltpu.make_async_copy(dzv.at[o], dz_ref.at[here, :], local_dz.at[k])

    owners = (mp, core, across, across_core)
    for k, o in enumerate(owners):
        if k > 0:
            arrived(coef.at[o], c_recv.at[o])
            if k != 2:
                for b in range(4):
                    arrived(tall.at[o, b], g_recv.at[o, b])
                arrived(zall.at[o], z_recv.at[o])
        stm[...] = jnp.concatenate([coef[o], jnp.zeros((block - 8, block), F32)], axis=0).T

        def dz_step(r, carry):
            rs = pl.ds(pl.multiple_of(r * CH, CH), CH)
            b, part = r * CH // sub, pl.ds(pl.multiple_of(r * CH % sub, CH), CH)
            both = stm[rs, :]
            dzv[o, rs, :] = (tall[o, b, part, :].astype(F32) * both[:, 0:1] - zall[o, rs, :] * both[:, 1:2]).astype(BF16)
            return carry

        lax.fori_loop(0, block // CH, dz_step, 0)
        dz_copy(k, o).start()

    for c in c_copies + q_copies + o_copies + [z_copy(k) for k in range(3)]:
        c.wait_send()
    for t in range(3):
        copy_a(t, 0).wait_send()
        for i in range(groups):
            if not (t == 2 and i == 1):
                copy_x(t, i).wait_send()

        @pl.when(mid)
        def _():
            copy_b(t, 0).wait_send()
            copy_b(t, 1).wait_send()
            copy_a(t, 2).wait_send()
            copy_a(t, 3).wait_send()

    copy_a(2, 1).wait_send()
    for i in range(groups):
        b = order[i]
        for d in range(1, groups):
            o = other_mp(d)
            remote(tsend.at[b, o], trecv.at[mp, b], t_send.at[i, d], t_recv.at[mp, b], mpd(o)).wait_send()
        for k in range(3):
            g_copy(i, k).wait_send()

        @pl.when(mp != b)
        def _():
            student_copy(b).wait_send()

        st_copy(i).wait()
        dz_copy(i, owners[i]).wait()


def grad_kernel(st_ref, dz_ref, out_ref, st, dz, out, load, dz_load, store):
    steps = st.shape[0]

    def rows(j):
        return pl.ds(pl.multiple_of(j * TILE, TILE), TILE)

    def fetch(j):
        return pltpu.make_async_copy(st_ref.at[rows(j), :], st.at[j], load.at[j])

    def put(j):
        return pltpu.make_async_copy(out.at[j], out_ref.at[rows(j), :], store.at[j])

    whole = pltpu.make_async_copy(dz_ref, dz, dz_load)
    whole.start()
    for j in range(steps):
        fetch(j).start()
    whole.wait()

    def step(j, carry):
        fetch(j).wait()
        out[j] = jnp.dot(st[j], dz[...], preferred_element_type=F32)
        put(j).start()
        return carry

    lax.fori_loop(0, steps, step, 0)
    for j in range(steps):
        put(j).wait()


def grad_matmul(st, dz):
    width, depth = st.shape
    cols = dz.shape[1]
    steps = width // TILE
    any_spec = pl.BlockSpec(memory_space=pl.ANY)
    dma = pltpu.SemaphoreType.DMA
    return pl.pallas_call(
        grad_kernel,
        in_specs=[any_spec, any_spec],
        out_specs=any_spec,
        out_shape=jax.ShapeDtypeStruct((width, cols), F32),
        scratch_shapes=[
            pltpu.VMEM((steps, TILE, depth), BF16),
            pltpu.VMEM((depth, cols), BF16),
            pltpu.VMEM((steps, TILE, cols), F32),
            dma((steps,)),
            dma(()),
            dma((steps,)),
        ],
        compiler_params=pltpu.CompilerParams(vmem_limit_bytes=56 * 1024 * 1024),
        name="grad",
    )(st, dz)


def fused_shards(total_rows, teacher_in, teacher_weight, student_in, projection, owner_order):
    rows, width = student_in.shape
    cols = projection.shape[1]
    block = owner_order.shape[0]
    groups = total_rows // block
    sub = block // groups
    any_spec = pl.BlockSpec(memory_space=pl.ANY)
    vmem_spec = pl.BlockSpec(memory_space=pltpu.VMEM)
    dma = pltpu.SemaphoreType.DMA
    cos, dz, st = pl.pallas_call(
        functools.partial(kernel, total_rows),
        out_shape=(
            jax.ShapeDtypeStruct((1, block), F32),
            jax.ShapeDtypeStruct((total_rows, cols), BF16),
            jax.ShapeDtypeStruct((width, total_rows), BF16),
        ),
        in_specs=[any_spec] * 4 + [vmem_spec],
        out_specs=(vmem_spec, any_spec, any_spec),
        scratch_shapes=[
            pltpu.VMEM((3, 4, 2, rows, width), BF16),
            pltpu.VMEM((3, width, cols), BF16),
            pltpu.VMEM((4, block, cols), F32),
            pltpu.VMEM((4, width, block), BF16),
            pltpu.VMEM((4, 1, block), jnp.int32),
            pltpu.VMEM((4, groups, sub, cols), BF16),
            pltpu.VMEM((4, groups, sub, cols), BF16),
            pltpu.VMEM((4, block, cols), BF16),
            pltpu.VMEM((4, block, cols), BF16),
            pltpu.VMEM((4, groups, sub, cols), BF16),
            pltpu.VMEM((4, block, cols), F32),
            pltpu.VMEM((4, block, cols), BF16),
            pltpu.VMEM((block, 128), F32),
            pltpu.VMEM((8, 8, 128), F32),
            pltpu.VMEM((4, 8, block), F32),
            dma((3, 4, 2)),
            dma((3, 4)),
            dma((3, 2)),
            dma((3, 4)),
            dma((3,)),
            dma((3,)),
            dma((4,)),
            dma((4,)),
            dma((4, 4)),
            dma((4, 4)),
            dma((4,)),
            dma((4,)),
            dma((8,)),
            dma((8,)),
            dma((4, 3)),
            dma((4, 4)),
            dma((3,)),
            dma((4,)),
            dma((4,)),
            dma((4,)),
            dma((4,)),
            dma((4,)),
        ],
        compiler_params=pltpu.CompilerParams(
            collective_id=0, has_side_effects=True, vmem_limit_bytes=56 * 1024 * 1024
        ),
        name="distill",
    )(teacher_in, teacher_weight, student_in, projection, owner_order.reshape(1, block))
    return grad_matmul(st, dz), cos.reshape(block)


def shards(teacher_in, teacher_weight, student_in, projection, owner_order):
    teacher_all = lax.all_gather(teacher_in, "dp", axis=0, tiled=True)
    student_all = lax.all_gather(student_in, "dp", axis=0, tiled=True)
    groups = lax.axis_size("mp")
    total_rows = teacher_all.shape[0]
    block_len = total_rows // groups
    sub_len = block_len // groups
    slab = teacher_all
    owned = lax.psum_scatter(
        jnp.dot(slab, teacher_weight, preferred_element_type=jnp.float32).astype(jnp.bfloat16),
        "mp",
        scatter_dimension=0,
        tiled=True,
    )
    picked = owned[owner_order].reshape(groups, sub_len, owned.shape[1])
    arrived = lax.all_to_all(picked, "mp", split_axis=0, concat_axis=0, tiled=True)
    target = arrived.reshape(block_len, owned.shape[1])
    slab = student_all
    student_out = lax.psum_scatter(
        jnp.dot(slab, projection, preferred_element_type=jnp.float32).astype(jnp.bfloat16),
        "mp",
        scatter_dimension=0,
        tiled=True,
    ).astype(jnp.float32)
    target_f = target.astype(jnp.float32)
    inner, sq_student, sq_target = lax.psum(
        (
            jnp.sum(student_out * target_f, axis=1),
            jnp.sum(student_out * student_out, axis=1),
            jnp.sum(target_f * target_f, axis=1),
        ),
        "dp",
    )
    inv_student = lax.rsqrt(sq_student + 1e-06)
    inv_target = lax.rsqrt(sq_target + 1e-06)
    cosine = inner * inv_student * inv_target
    scale = -1.0 / total_rows
    grad_out = scale * (
        target_f * (inv_student * inv_target)[:, None]
        - (inner * inv_target * inv_student**3)[:, None] * student_out
    )
    grad_out = grad_out.astype(jnp.bfloat16)
    projection_grad = lax.dot_general(
        student_all,
        lax.all_gather(grad_out, "mp", axis=0, tiled=True),
        (((0,), (0,)), ((), ())),
        preferred_element_type=jnp.float32,
    )
    return (projection_grad, cosine)


def solution(mesh):
    fits = mesh.shape["dp"] == 8 and mesh.shape["mp"] == 4

    def step(teacher_in, teacher_weight, student_in, projection, owner_order):
        args = (teacher_in, teacher_weight, student_in, projection, owner_order)
        if fits:
            return fused_shards(owner_order.shape[0] * mesh.shape["mp"], *args)
        return shards(*args)

    return jax.shard_map(
        step,
        mesh=mesh,
        in_specs=(P("dp", "mp"), P("mp", "dp"), P("dp", "mp"), P("mp", "dp"), P("mp")),
        out_specs=(P("mp", "dp"), P("mp")),
        check_vma=False,
    )
```

```python
import functools

import jax
import jax.numpy as jnp
from jax import lax
from jax.experimental import pallas as pl
from jax.experimental.pallas import tpu as pltpu
from jax.sharding import PartitionSpec as P

MESH = pl.DeviceIdType.MESH
F32 = jnp.float32
BF16 = jnp.bfloat16
TILE = 256


def kernel(
    total_rows,
    teacher_ref, weight_ref, student_ref, projection_ref, order_ref,
    cos_ref, dz_ref, st_ref,
    xbuf, wbuf, acc, stv, obuf, tsend, trecv, ssend, srecv, tall, zall, dzv, stm, statr, coef,
    x_recv, send_a, send_b, send_x, local_x, local_w, o_send, o_recv,
    t_send, t_recv, s_send, s_recv, q_send, q_recv, g_send, g_recv, z_send, z_recv, c_send, c_recv,
    local_st, local_dz,
):
    dp, mp = lax.axis_index("dp"), lax.axis_index("mp")
    z, x = dp // 2, dp % 2
    ox = 1 - x
    za = z + 1 - 2 * (z % 2)
    zb = 3 - z
    half = z // 2
    mid = (z + 1) // 2 == 1
    order = [z, za, 2 - half, 3 - 3 * half]
    rows, width = xbuf.shape[3], xbuf.shape[4]
    block = 2 * rows
    sub = tsend.shape[2]
    cols = wbuf.shape[2]
    tiles = cols // TILE
    groups = 4

    def at(plane, column):
        return (2 * plane + column, mp)

    def mpd(other):
        return (dp, other)

    def other_mp(d):
        return (mp + d) % groups

    def own_src(t):
        if t > 0:
            return teacher_ref.at[:, pl.ds((t - 1) * width, width)]
        return student_ref

    w_copies = []
    x_copies = []
    for t in range(3):
        x_copies.append(pltpu.make_async_copy(own_src(t), xbuf.at[t, z, x], local_x.at[t]))
        src = weight_ref.at[pl.ds((t - 1) * width, width), :] if t > 0 else projection_ref
        w_copies.append(pltpu.make_async_copy(src, wbuf.at[t], local_w.at[t]))
    for t in range(3):
        x_copies[t].start()
        w_copies[t].start()

    barrier = pltpu.get_barrier_semaphore()
    for d in range(1, 8):
        pl.semaphore_signal(barrier, inc=1, device_id=((dp + d) % 8, mp), device_id_type=MESH)
    for d in range(1, groups):
        pl.semaphore_signal(barrier, inc=1, device_id=mpd(other_mp(d)), device_id_type=MESH)
    pl.semaphore_wait(barrier, 7 + groups - 1)

    def remote(src, dst, ssem, rsem, device):
        return pltpu.make_async_remote_copy(
            src_ref=src, dst_ref=dst, send_sem=ssem, recv_sem=rsem,
            device_id=device, device_id_type=MESH,
        )

    def copy_x(t, i):
        src = own_src(t) if i == 0 else xbuf.at[t, order[i], x]
        return remote(src, xbuf.at[t, order[i], x], send_x.at[t, i], x_recv.at[t, order[i], x], at(z, ox))

    def copy_own(t, k):
        return remote(own_src(t), xbuf.at[t, z, x], send_a.at[t, k], x_recv.at[t, z, x], at(order[k], x))

    def copy_on(t):
        src = xbuf.at[t, zb, x]
        return remote(src, src, send_a.at[t, 0], x_recv.at[t, zb, x], at(za, x))

    def copy_swap(t):
        src = xbuf.at[t, z, ox]
        return remote(src, src, send_b.at[t], x_recv.at[t, z, ox], at(za, x))

    def wait_piece(t, s, c):
        pltpu.make_async_copy(xbuf.at[t, s, c], xbuf.at[t, s, c], x_recv.at[t, s, c]).wait()

    def own(t):
        copy_own(t, 1).start()
        copy_x(t, 0).start()
        copy_own(t, 2).start()

        @pl.when(jnp.logical_not(mid))
        def _():
            copy_own(t, 3).start()

    def event(t, i):
        wait_piece(t, order[i], x)
        if i == 2:

            @pl.when(mid)
            def _():
                copy_on(t).start()

        if not (t == 2 and i == 1):
            copy_x(t, i).start()

    def other(t, i):
        wait_piece(t, order[i], ox)
        if t == 2 and i == 0:
            copy_swap(t).start()

    bases = [2 * half, 2 - 2 * half]

    def dot_pair(t, p, cs):
        left = xbuf[t, pl.ds(bases[p], 2)].reshape(2 * block, width)
        return jnp.dot(left, wbuf[t, :, cs], preferred_element_type=F32)

    def tile_loop(body):
        def step(j, carry):
            body(pl.ds(pl.multiple_of(j * TILE, TILE), TILE))
            return carry

        lax.fori_loop(0, tiles, step, 0)

    def spread(b):
        hit = lax.broadcasted_iota(jnp.int32, (block, block), 0) == jnp.broadcast_to(obuf[b], (block, block))
        return jnp.where(hit, 1.0, 0.0).astype(BF16)

    def permute(b, part, cs):
        picked = lax.dot_general(spread(b), part, (((0,), (0,)), ((), ())), preferred_element_type=F32)
        tsend[b, :, :, cs] = picked.astype(BF16).reshape(groups, sub, TILE)

    def teacher_send(i):
        b = order[i]
        for d in range(1, groups):
            o = other_mp(d)
            remote(tsend.at[b, o], trecv.at[mp, b], t_send.at[i, d], t_recv.at[mp, b], mpd(o)).start()

    def teacher_first(p):
        def body(cs):
            acc[pl.ds(bases[p], 2), :, cs] = dot_pair(1, p, cs).reshape(2, block, TILE)

        tile_loop(body)

    def teacher_second(i):
        b = order[i]

        def body(cs):
            new = jnp.dot(xbuf[2, b].reshape(block, width), wbuf[2, :, cs], preferred_element_type=F32)
            permute(b, (acc[b, :, cs] + new).astype(BF16), cs)

        tile_loop(body)
        teacher_send(i)

    def student_copy(b):
        return remote(ssend.at[b], srecv.at[mp], s_send.at[b], s_recv.at[mp], mpd(b))

    def student(p):
        def body(cs):
            ssend[pl.ds(bases[p], 2), :, cs] = dot_pair(0, p, cs).astype(BF16).reshape(2, block, TILE)

        tile_loop(body)
        for i in (2 * p, 2 * p + 1):
            b = order[i]

            @pl.when(mp != b)
            def _():
                student_copy(b).start()

    def st_copy(i):
        b = order[i]
        return pltpu.make_async_copy(
            stv.at[b], st_ref.at[:, pl.ds(pl.multiple_of(b * block, block), block)], local_st.at[i]
        )

    def transpose(i):
        b = order[i]

        def step(j, carry):
            ks = pl.ds(pl.multiple_of(j * TILE, TILE), TILE)
            stv[b, ks, :] = xbuf[0, b, :, :, ks].reshape(block, TILE).T
            return carry

        lax.fori_loop(0, width // TILE, step, 0)
        st_copy(i).start()

    obuf[mp] = order_ref[...]
    o_copies = [
        remote(order_ref, obuf.at[mp], o_send.at[d], o_recv.at[mp], mpd(other_mp(d))) for d in range(1, groups)
    ]

    CH = 16
    core = mp + 1 - 2 * (mp % 2)
    across = (mp + 2) % 4
    across_core = (core + 2) % 4

    def arrived(ref, sem):
        pltpu.make_async_copy(ref, ref, sem).wait()

    def z_copy(k):
        o, to = ((mp, across), (mp, core), (across, core))[k]
        return remote(zall.at[o], zall.at[o], z_send.at[k], z_recv.at[o], mpd(to))

    def student_sum():
        for d in range(1, groups):
            o = other_mp(d)
            arrived(srecv.at[o], s_recv.at[o])

        def step(r, carry):
            rs = pl.ds(pl.multiple_of(r * CH, CH), CH)
            total = ssend[mp, rs, :].astype(F32)
            for d in range(1, groups):
                total = total + srecv[other_mp(d), rs, :].astype(F32)
            zall[mp, rs, :] = total
            return carry

        lax.fori_loop(0, block // CH, step, 0)
        z_copy(0).start()
        z_copy(1).start()

    def student_relay():
        arrived(zall.at[across], z_recv.at[across])
        z_copy(2).start()

    def g_copy(i, k):
        b = order[i]
        o, to = ((mp, across), (mp, core), (across, core))[k]
        return remote(tall.at[o, b], tall.at[o, b], g_send.at[i, k], g_recv.at[o, b], mpd(to))

    def target_sum(i):
        b = order[i]
        for d in range(1, groups):
            o = other_mp(d)
            arrived(trecv.at[o, b], t_recv.at[o, b])
        for r in range(sub // CH):
            rs = pl.ds(r * CH, CH)
            total = tsend[b, mp, rs, :].astype(F32)
            for d in range(1, groups):
                total = total + trecv[other_mp(d), b, rs, :].astype(F32)
            tall[mp, b, rs, :] = total.astype(BF16)
        g_copy(i, 0).start()
        g_copy(i, 1).start()
        for r in range(sub // CH):
            rows_here = pl.ds(pl.multiple_of(b * sub + r * CH, CH), CH)
            tt = tall[mp, b, pl.ds(r * CH, CH), :].astype(F32)
            zz = zall[mp, rows_here, :]
            lane = lax.broadcasted_iota(jnp.int32, (CH, 128), 1)
            s0 = jnp.sum(zz * tt, axis=1, keepdims=True)
            s1 = jnp.sum(zz * zz, axis=1, keepdims=True)
            s2 = jnp.sum(tt * tt, axis=1, keepdims=True)
            stm[rows_here, :] = jnp.where(lane == 0, s0, jnp.where(lane == 1, s1, jnp.where(lane == 2, s2, 0.0)))

    def target_relay(i):
        b = order[i]
        arrived(tall.at[across, b], g_recv.at[across, b])
        g_copy(i, 2).start()

    own(0)
    for c in o_copies:
        c.start()
    own(1)
    event(0, 1)
    event(1, 1)
    event(0, 2)
    event(0, 3)
    own(2)
    x_copies[0].wait()
    w_copies[0].wait()
    other(0, 0)
    other(0, 1)
    student(0)
    x_copies[1].wait()
    w_copies[1].wait()
    other(1, 0)
    other(1, 1)
    teacher_first(0)
    event(1, 2)
    event(1, 3)
    other(0, 2)
    other(0, 3)
    student(1)
    x_copies[2].wait()
    w_copies[2].wait()
    for d in range(1, groups):
        o = other_mp(d)
        arrived(obuf.at[o], o_recv.at[o])
    other(2, 0)
    event(2, 2)
    teacher_second(0)
    student_sum()
    event(2, 3)
    transpose(0)
    transpose(1)
    transpose(2)
    transpose(3)
    student_relay()
    other(1, 2)
    other(1, 3)
    teacher_first(1)
    event(2, 1)
    other(2, 1)
    teacher_second(1)
    target_sum(0)
    target_sum(1)
    other(2, 2)
    teacher_second(2)
    target_relay(0)
    target_relay(1)
    other(2, 3)
    teacher_second(3)
    target_sum(2)
    target_sum(3)

    statr[dp] = stm[...].T[0:8, :]
    q_copies = []
    for d in range(1, 8):
        o = (dp + d) % 8
        q_copies.append(remote(statr.at[dp], statr.at[dp], q_send.at[d], q_recv.at[dp], (o, mp)))
    for c in q_copies:
        c.start()
    target_relay(2)
    target_relay(3)
    for d in range(1, 8):
        o = (dp + d) % 8
        arrived(statr.at[o], q_recv.at[o])
    sums = statr[0]
    for s in range(1, 8):
        sums = sums + statr[s]
    inner = sums[0:1, :]
    inv_s = lax.rsqrt(sums[1:2, :] + 1e-06)
    inv_t = lax.rsqrt(sums[2:3, :] + 1e-06)
    cos_ref[...] = inner * inv_s * inv_t
    scale = -1.0 / total_rows
    on_target = jnp.broadcast_to(scale * (inv_s * inv_t), (8, block))
    on_student = jnp.broadcast_to(scale * (inner * inv_t * inv_s * inv_s * inv_s), (8, block))
    row = lax.broadcasted_iota(jnp.int32, (8, block), 0)
    coef[mp] = jnp.where(row == 0, on_target, jnp.where(row == 1, on_student, 0.0))
    c_copies = [
        remote(coef.at[mp], coef.at[mp], c_send.at[d], c_recv.at[mp], mpd(other_mp(d))) for d in range(1, groups)
    ]
    for c in c_copies:
        c.start()

    def dz_copy(k, o):
        here = pl.ds(pl.multiple_of(o * block, block), block)
        return pltpu.make_async_copy(dzv.at[o], dz_ref.at[here, :], local_dz.at[k])

    owners = (mp, core, across, across_core)
    for k, o in enumerate(owners):
        if k > 0:
            arrived(coef.at[o], c_recv.at[o])
            if k != 2:
                for b in range(4):
                    arrived(tall.at[o, b], g_recv.at[o, b])
                arrived(zall.at[o], z_recv.at[o])
        stm[...] = jnp.concatenate([coef[o], jnp.zeros((block - 8, block), F32)], axis=0).T

        def dz_step(r, carry):
            rs = pl.ds(pl.multiple_of(r * CH, CH), CH)
            b, part = r * CH // sub, pl.ds(pl.multiple_of(r * CH % sub, CH), CH)
            both = stm[rs, :]
            dzv[o, rs, :] = (tall[o, b, part, :].astype(F32) * both[:, 0:1] - zall[o, rs, :] * both[:, 1:2]).astype(BF16)
            return carry

        lax.fori_loop(0, block // CH, dz_step, 0)
        dz_copy(k, o).start()

    for c in c_copies + q_copies + o_copies + [z_copy(k) for k in range(3)]:
        c.wait_send()
    for t in range(3):
        copy_own(t, 1).wait_send()
        copy_own(t, 2).wait_send()
        for i in range(groups):
            if not (t == 2 and i == 1):
                copy_x(t, i).wait_send()

        @pl.when(mid)
        def _():
            copy_on(t).wait_send()

        @pl.when(jnp.logical_not(mid))
        def _():
            copy_own(t, 3).wait_send()

    copy_swap(2).wait_send()
    for i in range(groups):
        b = order[i]
        for d in range(1, groups):
            o = other_mp(d)
            remote(tsend.at[b, o], trecv.at[mp, b], t_send.at[i, d], t_recv.at[mp, b], mpd(o)).wait_send()
        for k in range(3):
            g_copy(i, k).wait_send()

        @pl.when(mp != b)
        def _():
            student_copy(b).wait_send()

        st_copy(i).wait()
        dz_copy(i, owners[i]).wait()


def grad_kernel(st_ref, dz_ref, out_ref, st, dz, out, load, dz_load, store):
    steps = st.shape[0]

    def rows(j):
        return pl.ds(pl.multiple_of(j * TILE, TILE), TILE)

    def fetch(j):
        return pltpu.make_async_copy(st_ref.at[rows(j), :], st.at[j], load.at[j])

    def put(j):
        return pltpu.make_async_copy(out.at[j], out_ref.at[rows(j), :], store.at[j])

    whole = pltpu.make_async_copy(dz_ref, dz, dz_load)
    whole.start()
    for j in range(steps):
        fetch(j).start()
    whole.wait()

    def step(j, carry):
        fetch(j).wait()
        out[j] = jnp.dot(st[j], dz[...], preferred_element_type=F32)
        put(j).start()
        return carry

    lax.fori_loop(0, steps, step, 0)
    for j in range(steps):
        put(j).wait()


def grad_matmul(st, dz):
    width, depth = st.shape
    cols = dz.shape[1]
    steps = width // TILE
    any_spec = pl.BlockSpec(memory_space=pl.ANY)
    dma = pltpu.SemaphoreType.DMA
    return pl.pallas_call(
        grad_kernel,
        in_specs=[any_spec, any_spec],
        out_specs=any_spec,
        out_shape=jax.ShapeDtypeStruct((width, cols), F32),
        scratch_shapes=[
            pltpu.VMEM((steps, TILE, depth), BF16),
            pltpu.VMEM((depth, cols), BF16),
            pltpu.VMEM((steps, TILE, cols), F32),
            dma((steps,)),
            dma(()),
            dma((steps,)),
        ],
        compiler_params=pltpu.CompilerParams(vmem_limit_bytes=56 * 1024 * 1024),
        name="grad",
    )(st, dz)


def fused_shards(total_rows, teacher_in, teacher_weight, student_in, projection, owner_order):
    rows, width = student_in.shape
    cols = projection.shape[1]
    block = owner_order.shape[0]
    groups = total_rows // block
    sub = block // groups
    any_spec = pl.BlockSpec(memory_space=pl.ANY)
    vmem_spec = pl.BlockSpec(memory_space=pltpu.VMEM)
    dma = pltpu.SemaphoreType.DMA
    cos, dz, st = pl.pallas_call(
        functools.partial(kernel, total_rows),
        out_shape=(
            jax.ShapeDtypeStruct((1, block), F32),
            jax.ShapeDtypeStruct((total_rows, cols), BF16),
            jax.ShapeDtypeStruct((width, total_rows), BF16),
        ),
        in_specs=[any_spec] * 4 + [vmem_spec],
        out_specs=(vmem_spec, any_spec, any_spec),
        scratch_shapes=[
            pltpu.VMEM((3, 4, 2, rows, width), BF16),
            pltpu.VMEM((3, width, cols), BF16),
            pltpu.VMEM((4, block, cols), F32),
            pltpu.VMEM((4, width, block), BF16),
            pltpu.VMEM((4, 1, block), jnp.int32),
            pltpu.VMEM((4, groups, sub, cols), BF16),
            pltpu.VMEM((4, groups, sub, cols), BF16),
            pltpu.VMEM((4, block, cols), BF16),
            pltpu.VMEM((4, block, cols), BF16),
            pltpu.VMEM((4, groups, sub, cols), BF16),
            pltpu.VMEM((4, block, cols), F32),
            pltpu.VMEM((4, block, cols), BF16),
            pltpu.VMEM((block, 128), F32),
            pltpu.VMEM((8, 8, 128), F32),
            pltpu.VMEM((4, 8, block), F32),
            dma((3, 4, 2)),
            dma((3, 4)),
            dma((3,)),
            dma((3, 4)),
            dma((3,)),
            dma((3,)),
            dma((4,)),
            dma((4,)),
            dma((4, 4)),
            dma((4, 4)),
            dma((4,)),
            dma((4,)),
            dma((8,)),
            dma((8,)),
            dma((4, 3)),
            dma((4, 4)),
            dma((3,)),
            dma((4,)),
            dma((4,)),
            dma((4,)),
            dma((4,)),
            dma((4,)),
        ],
        compiler_params=pltpu.CompilerParams(
            collective_id=0, has_side_effects=True, vmem_limit_bytes=56 * 1024 * 1024
        ),
        name="distill",
    )(teacher_in, teacher_weight, student_in, projection, owner_order.reshape(1, block))
    return grad_matmul(st, dz), cos.reshape(block)


def shards(teacher_in, teacher_weight, student_in, projection, owner_order):
    teacher_all = lax.all_gather(teacher_in, "dp", axis=0, tiled=True)
    student_all = lax.all_gather(student_in, "dp", axis=0, tiled=True)
    groups = lax.axis_size("mp")
    total_rows = teacher_all.shape[0]
    block_len = total_rows // groups
    sub_len = block_len // groups
    slab = teacher_all
    owned = lax.psum_scatter(
        jnp.dot(slab, teacher_weight, preferred_element_type=jnp.float32).astype(jnp.bfloat16),
        "mp",
        scatter_dimension=0,
        tiled=True,
    )
    picked = owned[owner_order].reshape(groups, sub_len, owned.shape[1])
    arrived = lax.all_to_all(picked, "mp", split_axis=0, concat_axis=0, tiled=True)
    target = arrived.reshape(block_len, owned.shape[1])
    slab = student_all
    student_out = lax.psum_scatter(
        jnp.dot(slab, projection, preferred_element_type=jnp.float32).astype(jnp.bfloat16),
        "mp",
        scatter_dimension=0,
        tiled=True,
    ).astype(jnp.float32)
    target_f = target.astype(jnp.float32)
    inner, sq_student, sq_target = lax.psum(
        (
            jnp.sum(student_out * target_f, axis=1),
            jnp.sum(student_out * student_out, axis=1),
            jnp.sum(target_f * target_f, axis=1),
        ),
        "dp",
    )
    inv_student = lax.rsqrt(sq_student + 1e-06)
    inv_target = lax.rsqrt(sq_target + 1e-06)
    cosine = inner * inv_student * inv_target
    scale = -1.0 / total_rows
    grad_out = scale * (
        target_f * (inv_student * inv_target)[:, None]
        - (inner * inv_target * inv_student**3)[:, None] * student_out
    )
    grad_out = grad_out.astype(jnp.bfloat16)
    projection_grad = lax.dot_general(
        student_all,
        lax.all_gather(grad_out, "mp", axis=0, tiled=True),
        (((0,), (0,)), ((), ())),
        preferred_element_type=jnp.float32,
    )
    return (projection_grad, cosine)


def solution(mesh):
    fits = mesh.shape["dp"] == 8 and mesh.shape["mp"] == 4

    def step(teacher_in, teacher_weight, student_in, projection, owner_order):
        args = (teacher_in, teacher_weight, student_in, projection, owner_order)
        if fits:
            return fused_shards(owner_order.shape[0] * mesh.shape["mp"], *args)
        return shards(*args)

    return jax.shard_map(
        step,
        mesh=mesh,
        in_specs=(P("dp", "mp"), P("mp", "dp"), P("dp", "mp"), P("mp", "dp"), P("mp")),
        out_specs=(P("mp", "dp"), P("mp")),
        check_vma=False,
    )
```

```python
import functools

import jax
import jax.numpy as jnp
from jax import lax
from jax.experimental import pallas as pl
from jax.experimental.pallas import tpu as pltpu
from jax.sharding import PartitionSpec as P

MESH = pl.DeviceIdType.MESH
F32 = jnp.float32
BF16 = jnp.bfloat16
TILE = 256


def kernel(
    total_rows,
    teacher_ref, weight_ref, student_ref, projection_ref, order_ref,
    cos_ref, dz_ref, st_ref,
    xbuf, wbuf, acc, stv, obuf, tsend, trecv, ssend, srecv, tall, zall, dzv, stm, statr, coef,
    x_recv, send_a, send_b, send_x, local_x, local_w, o_send, o_recv,
    t_send, t_recv, s_send, s_recv, q_send, q_recv, g_send, g_recv, z_send, z_recv, c_send, c_recv,
    local_st, local_dz,
):
    dp, mp = lax.axis_index("dp"), lax.axis_index("mp")
    z, x = dp // 2, dp % 2
    ox = 1 - x
    za = z + 1 - 2 * (z % 2)
    zb = 3 - z
    half = z // 2
    mid = (z + 1) // 2 == 1
    order = [z, za, 2 - half, 3 - 3 * half]
    rows, width = xbuf.shape[3], xbuf.shape[4]
    block = 2 * rows
    sub = tsend.shape[2]
    cols = wbuf.shape[2]
    tiles = cols // TILE
    groups = 4

    def at(plane, column):
        return (2 * plane + column, mp)

    def mpd(other):
        return (dp, other)

    def other_mp(d):
        return (mp + d) % groups

    def own_src(t):
        if t > 0:
            return teacher_ref.at[:, pl.ds((t - 1) * width, width)]
        return student_ref

    w_copies = []
    x_copies = []
    for t in range(3):
        x_copies.append(pltpu.make_async_copy(own_src(t), xbuf.at[t, z, x], local_x.at[t]))
        src = weight_ref.at[pl.ds((t - 1) * width, width), :] if t > 0 else projection_ref
        w_copies.append(pltpu.make_async_copy(src, wbuf.at[t], local_w.at[t]))
    for t in range(3):
        x_copies[t].start()
        w_copies[t].start()

    barrier = pltpu.get_barrier_semaphore()
    for d in range(1, 8):
        pl.semaphore_signal(barrier, inc=1, device_id=((dp + d) % 8, mp), device_id_type=MESH)
    for d in range(1, groups):
        pl.semaphore_signal(barrier, inc=1, device_id=mpd(other_mp(d)), device_id_type=MESH)
    pl.semaphore_wait(barrier, 7 + groups - 1)

    def remote(src, dst, ssem, rsem, device):
        return pltpu.make_async_remote_copy(
            src_ref=src, dst_ref=dst, send_sem=ssem, recv_sem=rsem,
            device_id=device, device_id_type=MESH,
        )

    def copy_x(t, i):
        src = own_src(t) if i == 0 else xbuf.at[t, order[i], x]
        return remote(src, xbuf.at[t, order[i], x], send_x.at[t, i], x_recv.at[t, order[i], x], at(z, ox))

    def copy_a(t, i):
        if i == 1:
            src, s, c = xbuf.at[t, z, ox], z, ox
        else:
            s, c = order[i], x
            src = own_src(t) if i == 0 else xbuf.at[t, s, c]
        return remote(src, xbuf.at[t, s, c], send_a.at[t, i], x_recv.at[t, s, c], at(za, x))

    def copy_b(t, i):
        s = order[i]
        src = own_src(t) if i == 0 else xbuf.at[t, s, x]
        return remote(src, xbuf.at[t, s, x], send_b.at[t, i], x_recv.at[t, s, x], at(zb, x))

    def wait_piece(t, s, c):
        pltpu.make_async_copy(xbuf.at[t, s, c], xbuf.at[t, s, c], x_recv.at[t, s, c]).wait()

    def if_mid(copy, flag=True):
        @pl.when(mid if flag else jnp.logical_not(mid))
        def _():
            copy.start()

    def event(t, i):
        wait_piece(t, order[i], x)
        if_mid(copy_b(t, 1) if i == 1 else copy_a(t, i))
        if not (t == 2 and i == 1):
            copy_x(t, i).start()

    def other(t, i):
        wait_piece(t, order[i], ox)

    bases = [2 * half, 2 - 2 * half]

    def dot_pair(t, p, cs):
        left = xbuf[t, pl.ds(bases[p], 2)].reshape(2 * block, width)
        return jnp.dot(left, wbuf[t, :, cs], preferred_element_type=F32)

    def tile_loop(body):
        def step(j, carry):
            body(pl.ds(pl.multiple_of(j * TILE, TILE), TILE))
            return carry

        lax.fori_loop(0, tiles, step, 0)

    def spread(b):
        hit = lax.broadcasted_iota(jnp.int32, (block, block), 0) == jnp.broadcast_to(obuf[b], (block, block))
        return jnp.where(hit, 1.0, 0.0).astype(BF16)

    def permute(b, part, cs):
        picked = lax.dot_general(spread(b), part, (((0,), (0,)), ((), ())), preferred_element_type=F32)
        tsend[b, :, :, cs] = picked.astype(BF16).reshape(groups, sub, TILE)

    def teacher_send(i):
        b = order[i]
        for d in range(1, groups):
            o = other_mp(d)
            remote(tsend.at[b, o], trecv.at[mp, b], t_send.at[i, d], t_recv.at[mp, b], mpd(o)).start()

    def teacher_first(p):
        def body(cs):
            acc[pl.ds(bases[p], 2), :, cs] = dot_pair(1, p, cs).reshape(2, block, TILE)

        tile_loop(body)

    def teacher_second(i):
        b = order[i]

        def body(cs):
            new = jnp.dot(xbuf[2, b].reshape(block, width), wbuf[2, :, cs], preferred_element_type=F32)
            permute(b, (acc[b, :, cs] + new).astype(BF16), cs)

        tile_loop(body)
        teacher_send(i)

    def student_copy(b):
        return remote(ssend.at[b], srecv.at[mp], s_send.at[b], s_recv.at[mp], mpd(b))

    def student(p):
        def body(cs):
            ssend[pl.ds(bases[p], 2), :, cs] = dot_pair(0, p, cs).astype(BF16).reshape(2, block, TILE)

        tile_loop(body)
        for i in (2 * p, 2 * p + 1):
            b = order[i]

            @pl.when(mp != b)
            def _():
                student_copy(b).start()

    def st_copy(i):
        b = order[i]
        return pltpu.make_async_copy(
            stv.at[b], st_ref.at[:, pl.ds(pl.multiple_of(b * block, block), block)], local_st.at[i]
        )

    def transpose(i):
        b = order[i]

        def step(j, carry):
            ks = pl.ds(pl.multiple_of(j * TILE, TILE), TILE)
            stv[b, ks, :] = xbuf[0, b, :, :, ks].reshape(block, TILE).T
            return carry

        lax.fori_loop(0, width // TILE, step, 0)
        st_copy(i).start()

    obuf[mp] = order_ref[...]
    o_copies = [
        remote(order_ref, obuf.at[mp], o_send.at[d], o_recv.at[mp], mpd(other_mp(d))) for d in range(1, groups)
    ]

    CH = 16
    core = mp + 1 - 2 * (mp % 2)
    across = (mp + 2) % 4
    across_core = (core + 2) % 4

    def arrived(ref, sem):
        pltpu.make_async_copy(ref, ref, sem).wait()

    def z_copy(k):
        o, to = ((mp, across), (mp, core), (across, core))[k]
        return remote(zall.at[o], zall.at[o], z_send.at[k], z_recv.at[o], mpd(to))

    def student_sum():
        for d in range(1, groups):
            o = other_mp(d)
            arrived(srecv.at[o], s_recv.at[o])

        def step(r, carry):
            rs = pl.ds(pl.multiple_of(r * CH, CH), CH)
            total = ssend[mp, rs, :].astype(F32)
            for d in range(1, groups):
                total = total + srecv[other_mp(d), rs, :].astype(F32)
            zall[mp, rs, :] = total
            return carry

        lax.fori_loop(0, block // CH, step, 0)
        z_copy(0).start()
        z_copy(1).start()

    def student_relay():
        arrived(zall.at[across], z_recv.at[across])
        z_copy(2).start()

    def g_copy(i, k):
        b = order[i]
        o, to = ((mp, across), (mp, core), (across, core))[k]
        return remote(tall.at[o, b], tall.at[o, b], g_send.at[i, k], g_recv.at[o, b], mpd(to))

    def target_sum(i):
        b = order[i]
        for d in range(1, groups):
            o = other_mp(d)
            arrived(trecv.at[o, b], t_recv.at[o, b])
        for r in range(sub // CH):
            rs = pl.ds(r * CH, CH)
            total = tsend[b, mp, rs, :].astype(F32)
            for d in range(1, groups):
                total = total + trecv[other_mp(d), b, rs, :].astype(F32)
            tall[mp, b, rs, :] = total.astype(BF16)
        g_copy(i, 0).start()
        g_copy(i, 1).start()
        for r in range(sub // CH):
            rows_here = pl.ds(pl.multiple_of(b * sub + r * CH, CH), CH)
            tt = tall[mp, b, pl.ds(r * CH, CH), :].astype(F32)
            zz = zall[mp, rows_here, :]
            lane = lax.broadcasted_iota(jnp.int32, (CH, 128), 1)
            s0 = jnp.sum(zz * tt, axis=1, keepdims=True)
            s1 = jnp.sum(zz * zz, axis=1, keepdims=True)
            s2 = jnp.sum(tt * tt, axis=1, keepdims=True)
            stm[rows_here, :] = jnp.where(lane == 0, s0, jnp.where(lane == 1, s1, jnp.where(lane == 2, s2, 0.0)))

    def target_relay(i):
        b = order[i]
        arrived(tall.at[across, b], g_recv.at[across, b])
        g_copy(i, 2).start()

    copy_a(0, 0).start()
    if_mid(copy_b(0, 0))
    for t in range(3):
        copy_x(t, 0).start()
    for c in o_copies:
        c.start()
    event(0, 1)
    if_mid(copy_a(1, 0), False)
    event(0, 2)
    if_mid(copy_b(1, 0))
    event(0, 3)
    if_mid(copy_a(1, 0))
    x_copies[0].wait()
    w_copies[0].wait()
    other(0, 0)
    event(1, 1)
    if_mid(copy_a(2, 0), False)
    other(0, 1)
    student(0)
    event(1, 2)
    if_mid(copy_b(2, 0))
    event(1, 3)
    other(0, 2)
    other(0, 3)
    student(1)

    @pl.when(mid)
    def _():
        wait_piece(2, order[1], x)
        copy_b(2, 1).start()

    event(2, 2)
    x_copies[1].wait()
    w_copies[1].wait()
    other(1, 0)
    other(1, 1)
    teacher_first(0)
    other(2, 0)
    event(2, 3)
    if_mid(copy_a(2, 0))
    copy_a(2, 1).start()
    x_copies[2].wait()
    w_copies[2].wait()
    for d in range(1, groups):
        o = other_mp(d)
        arrived(obuf.at[o], o_recv.at[o])
    teacher_second(0)
    student_sum()
    transpose(0)
    transpose(1)
    transpose(2)
    transpose(3)
    student_relay()
    other(1, 2)
    other(1, 3)
    teacher_first(1)

    @pl.when(jnp.logical_not(mid))
    def _():
        wait_piece(2, order[1], x)

    other(2, 1)
    teacher_second(1)
    target_sum(0)
    target_sum(1)
    other(2, 2)
    teacher_second(2)
    target_relay(0)
    target_relay(1)
    other(2, 3)
    teacher_second(3)
    target_sum(2)
    target_sum(3)

    statr[dp] = stm[...].T[0:8, :]
    q_copies = []
    for d in range(1, 8):
        o = (dp + d) % 8
        q_copies.append(remote(statr.at[dp], statr.at[dp], q_send.at[d], q_recv.at[dp], (o, mp)))
    for c in q_copies:
        c.start()
    target_relay(2)
    target_relay(3)
    for d in range(1, 8):
        o = (dp + d) % 8
        arrived(statr.at[o], q_recv.at[o])
    sums = statr[0]
    for s in range(1, 8):
        sums = sums + statr[s]
    inner = sums[0:1, :]
    inv_s = lax.rsqrt(sums[1:2, :] + 1e-06)
    inv_t = lax.rsqrt(sums[2:3, :] + 1e-06)
    cos_ref[...] = inner * inv_s * inv_t
    scale = -1.0 / total_rows
    on_target = jnp.broadcast_to(scale * (inv_s * inv_t), (8, block))
    on_student = jnp.broadcast_to(scale * (inner * inv_t * inv_s * inv_s * inv_s), (8, block))
    row = lax.broadcasted_iota(jnp.int32, (8, block), 0)
    coef[mp] = jnp.where(row == 0, on_target, jnp.where(row == 1, on_student, 0.0))
    c_copies = [
        remote(coef.at[mp], coef.at[mp], c_send.at[d], c_recv.at[mp], mpd(other_mp(d))) for d in range(1, groups)
    ]
    for c in c_copies:
        c.start()

    def dz_copy(k, o):
        here = pl.ds(pl.multiple_of(o * block, block), block)
        return pltpu.make_async_copy(dzv.at[o], dz_ref.at[here, :], local_dz.at[k])

    owners = (mp, core, across, across_core)
    for k, o in enumerate(owners):
        if k > 0:
            arrived(coef.at[o], c_recv.at[o])
            if k != 2:
                for b in range(4):
                    arrived(tall.at[o, b], g_recv.at[o, b])
                arrived(zall.at[o], z_recv.at[o])
        stm[...] = jnp.concatenate([coef[o], jnp.zeros((block - 8, block), F32)], axis=0).T

        def dz_step(r, carry):
            rs = pl.ds(pl.multiple_of(r * CH, CH), CH)
            b, part = r * CH // sub, pl.ds(pl.multiple_of(r * CH % sub, CH), CH)
            both = stm[rs, :]
            dzv[o, rs, :] = (tall[o, b, part, :].astype(F32) * both[:, 0:1] - zall[o, rs, :] * both[:, 1:2]).astype(BF16)
            return carry

        lax.fori_loop(0, block // CH, dz_step, 0)
        dz_copy(k, o).start()

    for c in c_copies + q_copies + o_copies + [z_copy(k) for k in range(3)]:
        c.wait_send()
    for t in range(3):
        copy_a(t, 0).wait_send()
        for i in range(groups):
            if not (t == 2 and i == 1):
                copy_x(t, i).wait_send()

        @pl.when(mid)
        def _():
            copy_b(t, 0).wait_send()
            copy_b(t, 1).wait_send()
            copy_a(t, 2).wait_send()
            copy_a(t, 3).wait_send()

    copy_a(2, 1).wait_send()
    for i in range(groups):
        b = order[i]
        for d in range(1, groups):
            o = other_mp(d)
            remote(tsend.at[b, o], trecv.at[mp, b], t_send.at[i, d], t_recv.at[mp, b], mpd(o)).wait_send()
        for k in range(3):
            g_copy(i, k).wait_send()

        @pl.when(mp != b)
        def _():
            student_copy(b).wait_send()

        st_copy(i).wait()
        dz_copy(i, owners[i]).wait()


def grad_kernel(st_ref, dz_ref, out_ref, st, dz, out, load, dz_load, store):
    steps = st.shape[0]

    def rows(j):
        return pl.ds(pl.multiple_of(j * TILE, TILE), TILE)

    def fetch(j):
        return pltpu.make_async_copy(st_ref.at[rows(j), :], st.at[j], load.at[j])

    def put(j):
        return pltpu.make_async_copy(out.at[j], out_ref.at[rows(j), :], store.at[j])

    whole = pltpu.make_async_copy(dz_ref, dz, dz_load)
    whole.start()
    for j in range(steps):
        fetch(j).start()
    whole.wait()

    def step(j, carry):
        fetch(j).wait()
        out[j] = jnp.dot(st[j], dz[...], preferred_element_type=F32)
        put(j).start()
        return carry

    lax.fori_loop(0, steps, step, 0)
    for j in range(steps):
        put(j).wait()


def grad_matmul(st, dz):
    width, depth = st.shape
    cols = dz.shape[1]
    steps = width // TILE
    any_spec = pl.BlockSpec(memory_space=pl.ANY)
    dma = pltpu.SemaphoreType.DMA
    return pl.pallas_call(
        grad_kernel,
        in_specs=[any_spec, any_spec],
        out_specs=any_spec,
        out_shape=jax.ShapeDtypeStruct((width, cols), F32),
        scratch_shapes=[
            pltpu.VMEM((steps, TILE, depth), BF16),
            pltpu.VMEM((depth, cols), BF16),
            pltpu.VMEM((steps, TILE, cols), F32),
            dma((steps,)),
            dma(()),
            dma((steps,)),
        ],
        compiler_params=pltpu.CompilerParams(vmem_limit_bytes=56 * 1024 * 1024),
        name="grad",
    )(st, dz)


def fused_shards(total_rows, teacher_in, teacher_weight, student_in, projection, owner_order):
    rows, width = student_in.shape
    cols = projection.shape[1]
    block = owner_order.shape[0]
    groups = total_rows // block
    sub = block // groups
    any_spec = pl.BlockSpec(memory_space=pl.ANY)
    vmem_spec = pl.BlockSpec(memory_space=pltpu.VMEM)
    dma = pltpu.SemaphoreType.DMA
    cos, dz, st = pl.pallas_call(
        functools.partial(kernel, total_rows),
        out_shape=(
            jax.ShapeDtypeStruct((1, block), F32),
            jax.ShapeDtypeStruct((total_rows, cols), BF16),
            jax.ShapeDtypeStruct((width, total_rows), BF16),
        ),
        in_specs=[any_spec] * 4 + [vmem_spec],
        out_specs=(vmem_spec, any_spec, any_spec),
        scratch_shapes=[
            pltpu.VMEM((3, 4, 2, rows, width), BF16),
            pltpu.VMEM((3, width, cols), BF16),
            pltpu.VMEM((4, block, cols), F32),
            pltpu.VMEM((4, width, block), BF16),
            pltpu.VMEM((4, 1, block), jnp.int32),
            pltpu.VMEM((4, groups, sub, cols), BF16),
            pltpu.VMEM((4, groups, sub, cols), BF16),
            pltpu.VMEM((4, block, cols), BF16),
            pltpu.VMEM((4, block, cols), BF16),
            pltpu.VMEM((4, groups, sub, cols), BF16),
            pltpu.VMEM((4, block, cols), F32),
            pltpu.VMEM((4, block, cols), BF16),
            pltpu.VMEM((block, 128), F32),
            pltpu.VMEM((8, 8, 128), F32),
            pltpu.VMEM((4, 8, block), F32),
            dma((3, 4, 2)),
            dma((3, 4)),
            dma((3, 2)),
            dma((3, 4)),
            dma((3,)),
            dma((3,)),
            dma((4,)),
            dma((4,)),
            dma((4, 4)),
            dma((4, 4)),
            dma((4,)),
            dma((4,)),
            dma((8,)),
            dma((8,)),
            dma((4, 3)),
            dma((4, 4)),
            dma((3,)),
            dma((4,)),
            dma((4,)),
            dma((4,)),
            dma((4,)),
            dma((4,)),
        ],
        compiler_params=pltpu.CompilerParams(
            collective_id=0, has_side_effects=True, vmem_limit_bytes=56 * 1024 * 1024
        ),
        name="distill",
    )(teacher_in, teacher_weight, student_in, projection, owner_order.reshape(1, block))
    return grad_matmul(st, dz), cos.reshape(block)


def shards(teacher_in, teacher_weight, student_in, projection, owner_order):
    teacher_all = lax.all_gather(teacher_in, "dp", axis=0, tiled=True)
    student_all = lax.all_gather(student_in, "dp", axis=0, tiled=True)
    groups = lax.axis_size("mp")
    total_rows = teacher_all.shape[0]
    block_len = total_rows // groups
    sub_len = block_len // groups
    slab = teacher_all
    owned = lax.psum_scatter(
        jnp.dot(slab, teacher_weight, preferred_element_type=jnp.float32).astype(jnp.bfloat16),
        "mp",
        scatter_dimension=0,
        tiled=True,
    )
    picked = owned[owner_order].reshape(groups, sub_len, owned.shape[1])
    arrived = lax.all_to_all(picked, "mp", split_axis=0, concat_axis=0, tiled=True)
    target = arrived.reshape(block_len, owned.shape[1])
    slab = student_all
    student_out = lax.psum_scatter(
        jnp.dot(slab, projection, preferred_element_type=jnp.float32).astype(jnp.bfloat16),
        "mp",
        scatter_dimension=0,
        tiled=True,
    ).astype(jnp.float32)
    target_f = target.astype(jnp.float32)
    inner, sq_student, sq_target = lax.psum(
        (
            jnp.sum(student_out * target_f, axis=1),
            jnp.sum(student_out * student_out, axis=1),
            jnp.sum(target_f * target_f, axis=1),
        ),
        "dp",
    )
    inv_student = lax.rsqrt(sq_student + 1e-06)
    inv_target = lax.rsqrt(sq_target + 1e-06)
    cosine = inner * inv_student * inv_target
    scale = -1.0 / total_rows
    grad_out = scale * (
        target_f * (inv_student * inv_target)[:, None]
        - (inner * inv_target * inv_student**3)[:, None] * student_out
    )
    grad_out = grad_out.astype(jnp.bfloat16)
    projection_grad = lax.dot_general(
        student_all,
        lax.all_gather(grad_out, "mp", axis=0, tiled=True),
        (((0,), (0,)), ((), ())),
        preferred_element_type=jnp.float32,
    )
    return (projection_grad, cosine)


def solution(mesh):
    fits = mesh.shape["dp"] == 8 and mesh.shape["mp"] == 4

    def step(teacher_in, teacher_weight, student_in, projection, owner_order):
        args = (teacher_in, teacher_weight, student_in, projection, owner_order)
        if fits:
            return fused_shards(owner_order.shape[0] * mesh.shape["mp"], *args)
        return shards(*args)

    return jax.shard_map(
        step,
        mesh=mesh,
        in_specs=(P("dp", "mp"), P("mp", "dp"), P("dp", "mp"), P("mp", "dp"), P("mp")),
        out_specs=(P("mp", "dp"), P("mp")),
        check_vma=False,
    )
```

```python
import functools

import jax
import jax.numpy as jnp
from jax import lax
from jax.experimental import pallas as pl
from jax.experimental.pallas import tpu as pltpu
from jax.sharding import PartitionSpec as P

MESH = pl.DeviceIdType.MESH
F32 = jnp.float32
BF16 = jnp.bfloat16
TILE = 256


def kernel(
    total_rows,
    teacher_ref, weight_ref, student_ref, projection_ref, order_ref,
    cos_ref, dz_ref, st_ref,
    xbuf, wbuf, acc, stv, obuf, tsend, trecv, ssend, srecv, tall, zall, dzv, stm, statr, coef,
    x_recv, send_a, send_b, send_x, local_x, local_w, o_send, o_recv,
    t_send, t_recv, s_send, s_recv, q_send, q_recv, g_send, g_recv, z_send, z_recv, c_send, c_recv,
    local_st, local_dz,
):
    dp, mp = lax.axis_index("dp"), lax.axis_index("mp")
    z, x = dp // 2, dp % 2
    ox = 1 - x
    za = z + 1 - 2 * (z % 2)
    zb = 3 - z
    half = z // 2
    mid = (z + 1) // 2 == 1
    order = [z, za, 2 - half, 3 - 3 * half]
    rows, width = xbuf.shape[3], xbuf.shape[4]
    block = 2 * rows
    sub = tsend.shape[2]
    cols = wbuf.shape[2]
    tiles = cols // TILE
    groups = 4

    def at(plane, column):
        return (2 * plane + column, mp)

    def mpd(other):
        return (dp, other)

    def other_mp(d):
        return (mp + d) % groups

    def own_src(t):
        if t > 0:
            return teacher_ref.at[:, pl.ds((t - 1) * width, width)]
        return student_ref

    w_copies = []
    x_copies = []
    for t in range(3):
        x_copies.append(pltpu.make_async_copy(own_src(t), xbuf.at[t, z, x], local_x.at[t]))
        src = weight_ref.at[pl.ds((t - 1) * width, width), :] if t > 0 else projection_ref
        w_copies.append(pltpu.make_async_copy(src, wbuf.at[t], local_w.at[t]))
    for t in range(3):
        x_copies[t].start()
        w_copies[t].start()

    barrier = pltpu.get_barrier_semaphore()
    for d in range(1, 8):
        pl.semaphore_signal(barrier, inc=1, device_id=((dp + d) % 8, mp), device_id_type=MESH)
    for d in range(1, groups):
        pl.semaphore_signal(barrier, inc=1, device_id=mpd(other_mp(d)), device_id_type=MESH)
    pl.semaphore_wait(barrier, 7 + groups - 1)

    def remote(src, dst, ssem, rsem, device):
        return pltpu.make_async_remote_copy(
            src_ref=src, dst_ref=dst, send_sem=ssem, recv_sem=rsem,
            device_id=device, device_id_type=MESH,
        )

    def copy_x(t, i):
        src = own_src(t) if i == 0 else xbuf.at[t, order[i], x]
        return remote(src, xbuf.at[t, order[i], x], send_x.at[t, i], x_recv.at[t, order[i], x], at(z, ox))

    def copy_a(t, i):
        if i == 1:
            src, s, c = xbuf.at[t, z, ox], z, ox
        else:
            s, c = order[i], x
            src = own_src(t) if i == 0 else xbuf.at[t, s, c]
        return remote(src, xbuf.at[t, s, c], send_a.at[t, i], x_recv.at[t, s, c], at(za, x))

    def copy_b(t, i):
        s = order[i]
        src = own_src(t) if i == 0 else xbuf.at[t, s, x]
        return remote(src, xbuf.at[t, s, x], send_b.at[t, i], x_recv.at[t, s, x], at(zb, x))

    def wait_piece(t, s, c):
        pltpu.make_async_copy(xbuf.at[t, s, c], xbuf.at[t, s, c], x_recv.at[t, s, c]).wait()

    def own(t):
        copy_a(t, 0).start()

        @pl.when(mid)
        def _():
            copy_b(t, 0).start()

    def event(t, i):
        wait_piece(t, order[i], x)

        @pl.when(mid)
        def _():
            (copy_b(t, 1) if i == 1 else copy_a(t, i)).start()

        if not (t == 2 and i == 1):
            copy_x(t, i).start()

    def other(t, i):
        wait_piece(t, order[i], ox)
        if t == 2 and i == 0:
            copy_a(t, 1).start()

    def dot_block(t, b, cs):
        return jnp.dot(xbuf[t, b].reshape(block, width), wbuf[t, :, cs], preferred_element_type=F32)

    def tile_loop(body):
        def step(j, carry):
            body(pl.ds(pl.multiple_of(j * TILE, TILE), TILE))
            return carry

        lax.fori_loop(0, tiles, step, 0)

    def spread(b):
        hit = lax.broadcasted_iota(jnp.int32, (block, block), 0) == jnp.broadcast_to(obuf[b], (block, block))
        return jnp.where(hit, 1.0, 0.0).astype(BF16)

    def permute(b, part, cs):
        picked = lax.dot_general(spread(b), part, (((0,), (0,)), ((), ())), preferred_element_type=F32)
        tsend[b, :, :, cs] = picked.astype(BF16).reshape(groups, sub, TILE)

    def teacher_send(i):
        b = order[i]
        for d in range(1, groups):
            o = other_mp(d)
            remote(tsend.at[b, o], trecv.at[mp, b], t_send.at[i, d], t_recv.at[mp, b], mpd(o)).start()

    def teacher_first(i):
        b = order[i]

        def body(cs):
            acc[b, :, cs] = dot_block(1, b, cs)

        tile_loop(body)

    def teacher_second(i):
        b = order[i]

        def body(cs):
            permute(b, (acc[b, :, cs] + dot_block(2, b, cs)).astype(BF16), cs)

        tile_loop(body)
        teacher_send(i)

    def student_copy(b):
        return remote(ssend.at[b], srecv.at[mp], s_send.at[b], s_recv.at[mp], mpd(b))

    def student(i):
        b = order[i]

        def body(cs):
            ssend[b, :, cs] = dot_block(0, b, cs).astype(BF16)

        tile_loop(body)

        @pl.when(mp != b)
        def _():
            student_copy(b).start()

    def st_copy(i):
        b = order[i]
        return pltpu.make_async_copy(
            stv.at[b], st_ref.at[:, pl.ds(pl.multiple_of(b * block, block), block)], local_st.at[i]
        )

    def transpose(i):
        b = order[i]

        def step(j, carry):
            ks = pl.ds(pl.multiple_of(j * TILE, TILE), TILE)
            stv[b, ks, :] = xbuf[0, b, :, :, ks].reshape(block, TILE).T
            return carry

        lax.fori_loop(0, width // TILE, step, 0)
        st_copy(i).start()

    obuf[mp] = order_ref[...]
    o_copies = [
        remote(order_ref, obuf.at[mp], o_send.at[d], o_recv.at[mp], mpd(other_mp(d))) for d in range(1, groups)
    ]

    CH = 16
    core = mp + 1 - 2 * (mp % 2)
    across = (mp + 2) % 4
    across_core = (core + 2) % 4

    def arrived(ref, sem):
        pltpu.make_async_copy(ref, ref, sem).wait()

    def z_copy(k):
        o, to = ((mp, across), (mp, core), (across, core))[k]
        return remote(zall.at[o], zall.at[o], z_send.at[k], z_recv.at[o], mpd(to))

    def student_sum():
        for d in range(1, groups):
            o = other_mp(d)
            arrived(srecv.at[o], s_recv.at[o])

        def step(r, carry):
            rs = pl.ds(pl.multiple_of(r * CH, CH), CH)
            total = ssend[mp, rs, :].astype(F32)
            for d in range(1, groups):
                total = total + srecv[other_mp(d), rs, :].astype(F32)
            zall[mp, rs, :] = total
            return carry

        lax.fori_loop(0, block // CH, step, 0)
        z_copy(0).start()
        z_copy(1).start()

    def student_relay():
        arrived(zall.at[across], z_recv.at[across])
        z_copy(2).start()

    def g_copy(i, k):
        b = order[i]
        o, to = ((mp, across), (mp, core), (across, core))[k]
        return remote(tall.at[o, b], tall.at[o, b], g_send.at[i, k], g_recv.at[o, b], mpd(to))

    def target_sum(i):
        b = order[i]
        for d in range(1, groups):
            o = other_mp(d)
            arrived(trecv.at[o, b], t_recv.at[o, b])
        for r in range(sub // CH):
            rs = pl.ds(r * CH, CH)
            total = tsend[b, mp, rs, :].astype(F32)
            for d in range(1, groups):
                total = total + trecv[other_mp(d), b, rs, :].astype(F32)
            tall[mp, b, rs, :] = total.astype(BF16)
        g_copy(i, 0).start()
        g_copy(i, 1).start()
        for r in range(sub // CH):
            rows_here = pl.ds(pl.multiple_of(b * sub + r * CH, CH), CH)
            tt = tall[mp, b, pl.ds(r * CH, CH), :].astype(F32)
            zz = zall[mp, rows_here, :]
            lane = lax.broadcasted_iota(jnp.int32, (CH, 128), 1)
            s0 = jnp.sum(zz * tt, axis=1, keepdims=True)
            s1 = jnp.sum(zz * zz, axis=1, keepdims=True)
            s2 = jnp.sum(tt * tt, axis=1, keepdims=True)
            stm[rows_here, :] = jnp.where(lane == 0, s0, jnp.where(lane == 1, s1, jnp.where(lane == 2, s2, 0.0)))

    def target_relay(i):
        b = order[i]
        arrived(tall.at[across, b], g_recv.at[across, b])
        g_copy(i, 2).start()

    own(0)
    copy_x(0, 0).start()
    copy_x(1, 0).start()
    for c in o_copies:
        c.start()
    own(1)
    copy_x(2, 0).start()
    event(0, 1)
    x_copies[0].wait()
    w_copies[0].wait()
    other(0, 0)
    student(0)
    event(0, 2)
    event(1, 1)
    event(0, 3)
    x_copies[1].wait()
    w_copies[1].wait()
    other(1, 0)
    teacher_first(0)
    other(0, 1)
    student(1)
    event(1, 2)
    own(2)
    other(0, 2)
    student(2)
    event(1, 3)
    other(0, 3)
    student(3)
    event(2, 1)
    other(2, 0)
    other(1, 1)
    teacher_first(1)
    event(2, 2)
    student_sum()
    other(1, 2)
    teacher_first(2)
    x_copies[2].wait()
    w_copies[2].wait()
    for d in range(1, groups):
        o = other_mp(d)
        arrived(obuf.at[o], o_recv.at[o])
    teacher_second(0)
    event(2, 3)
    student_relay()
    other(1, 3)
    teacher_first(3)
    other(2, 1)
    teacher_second(1)
    target_sum(0)
    other(2, 2)
    teacher_second(2)
    target_sum(1)
    target_relay(0)
    other(2, 3)
    teacher_second(3)
    target_sum(2)
    target_relay(1)
    transpose(0)
    transpose(1)
    target_sum(3)

    statr[dp] = stm[...].T[0:8, :]
    q_copies = []
    for d in range(1, 8):
        o = (dp + d) % 8
        q_copies.append(remote(statr.at[dp], statr.at[dp], q_send.at[d], q_recv.at[dp], (o, mp)))
    for c in q_copies:
        c.start()
    target_relay(2)
    transpose(2)
    target_relay(3)
    transpose(3)
    for d in range(1, 8):
        o = (dp + d) % 8
        arrived(statr.at[o], q_recv.at[o])
    sums = statr[0]
    for s in range(1, 8):
        sums = sums + statr[s]
    inner = sums[0:1, :]
    inv_s = lax.rsqrt(sums[1:2, :] + 1e-06)
    inv_t = lax.rsqrt(sums[2:3, :] + 1e-06)
    cos_ref[...] = inner * inv_s * inv_t
    scale = -1.0 / total_rows
    on_target = jnp.broadcast_to(scale * (inv_s * inv_t), (8, block))
    on_student = jnp.broadcast_to(scale * (inner * inv_t * inv_s * inv_s * inv_s), (8, block))
    row = lax.broadcasted_iota(jnp.int32, (8, block), 0)
    coef[mp] = jnp.where(row == 0, on_target, jnp.where(row == 1, on_student, 0.0))
    c_copies = [
        remote(coef.at[mp], coef.at[mp], c_send.at[d], c_recv.at[mp], mpd(other_mp(d))) for d in range(1, groups)
    ]
    for c in c_copies:
        c.start()

    def dz_copy(k, o):
        here = pl.ds(pl.multiple_of(o * block, block), block)
        return pltpu.make_async_copy(dzv.at[o], dz_ref.at[here, :], local_dz.at[k])

    owners = (mp, core, across, across_core)
    for k, o in enumerate(owners):
        if k > 0:
            arrived(coef.at[o], c_recv.at[o])
            if k != 2:
                for b in range(4):
                    arrived(tall.at[o, b], g_recv.at[o, b])
                arrived(zall.at[o], z_recv.at[o])
        stm[...] = jnp.concatenate([coef[o], jnp.zeros((block - 8, block), F32)], axis=0).T

        def dz_step(r, carry):
            rs = pl.ds(pl.multiple_of(r * CH, CH), CH)
            b, part = r * CH // sub, pl.ds(pl.multiple_of(r * CH % sub, CH), CH)
            both = stm[rs, :]
            dzv[o, rs, :] = (tall[o, b, part, :].astype(F32) * both[:, 0:1] - zall[o, rs, :] * both[:, 1:2]).astype(BF16)
            return carry

        lax.fori_loop(0, block // CH, dz_step, 0)
        dz_copy(k, o).start()

    for c in c_copies + q_copies + o_copies + [z_copy(k) for k in range(3)]:
        c.wait_send()
    for t in range(3):
        copy_a(t, 0).wait_send()
        for i in range(groups):
            if not (t == 2 and i == 1):
                copy_x(t, i).wait_send()

        @pl.when(mid)
        def _():
            copy_b(t, 0).wait_send()
            copy_b(t, 1).wait_send()
            copy_a(t, 2).wait_send()
            copy_a(t, 3).wait_send()

    copy_a(2, 1).wait_send()
    for i in range(groups):
        b = order[i]
        for d in range(1, groups):
            o = other_mp(d)
            remote(tsend.at[b, o], trecv.at[mp, b], t_send.at[i, d], t_recv.at[mp, b], mpd(o)).wait_send()
        for k in range(3):
            g_copy(i, k).wait_send()

        @pl.when(mp != b)
        def _():
            student_copy(b).wait_send()

        st_copy(i).wait()
        dz_copy(i, owners[i]).wait()


def grad_kernel(st_ref, dz_ref, out_ref, st, dz, out, load, dz_load, store):
    steps = st.shape[0]

    def rows(j):
        return pl.ds(pl.multiple_of(j * TILE, TILE), TILE)

    def fetch(j):
        return pltpu.make_async_copy(st_ref.at[rows(j), :], st.at[j], load.at[j])

    def put(j):
        return pltpu.make_async_copy(out.at[j], out_ref.at[rows(j), :], store.at[j])

    whole = pltpu.make_async_copy(dz_ref, dz, dz_load)
    whole.start()
    for j in range(steps):
        fetch(j).start()
    whole.wait()

    def step(j, carry):
        fetch(j).wait()
        out[j] = jnp.dot(st[j], dz[...], preferred_element_type=F32)
        put(j).start()
        return carry

    lax.fori_loop(0, steps, step, 0)
    for j in range(steps):
        put(j).wait()


def grad_matmul(st, dz):
    width, depth = st.shape
    cols = dz.shape[1]
    steps = width // TILE
    any_spec = pl.BlockSpec(memory_space=pl.ANY)
    dma = pltpu.SemaphoreType.DMA
    return pl.pallas_call(
        grad_kernel,
        in_specs=[any_spec, any_spec],
        out_specs=any_spec,
        out_shape=jax.ShapeDtypeStruct((width, cols), F32),
        scratch_shapes=[
            pltpu.VMEM((steps, TILE, depth), BF16),
            pltpu.VMEM((depth, cols), BF16),
            pltpu.VMEM((steps, TILE, cols), F32),
            dma((steps,)),
            dma(()),
            dma((steps,)),
        ],
        compiler_params=pltpu.CompilerParams(vmem_limit_bytes=56 * 1024 * 1024),
        name="grad",
    )(st, dz)


def fused_shards(total_rows, teacher_in, teacher_weight, student_in, projection, owner_order):
    rows, width = student_in.shape
    cols = projection.shape[1]
    block = owner_order.shape[0]
    groups = total_rows // block
    sub = block // groups
    any_spec = pl.BlockSpec(memory_space=pl.ANY)
    vmem_spec = pl.BlockSpec(memory_space=pltpu.VMEM)
    dma = pltpu.SemaphoreType.DMA
    cos, dz, st = pl.pallas_call(
        functools.partial(kernel, total_rows),
        out_shape=(
            jax.ShapeDtypeStruct((1, block), F32),
            jax.ShapeDtypeStruct((total_rows, cols), BF16),
            jax.ShapeDtypeStruct((width, total_rows), BF16),
        ),
        in_specs=[any_spec] * 4 + [vmem_spec],
        out_specs=(vmem_spec, any_spec, any_spec),
        scratch_shapes=[
            pltpu.VMEM((3, 4, 2, rows, width), BF16),
            pltpu.VMEM((3, width, cols), BF16),
            pltpu.VMEM((4, block, cols), F32),
            pltpu.VMEM((4, width, block), BF16),
            pltpu.VMEM((4, 1, block), jnp.int32),
            pltpu.VMEM((4, groups, sub, cols), BF16),
            pltpu.VMEM((4, groups, sub, cols), BF16),
            pltpu.VMEM((4, block, cols), BF16),
            pltpu.VMEM((4, block, cols), BF16),
            pltpu.VMEM((4, groups, sub, cols), BF16),
            pltpu.VMEM((4, block, cols), F32),
            pltpu.VMEM((4, block, cols), BF16),
            pltpu.VMEM((block, 128), F32),
            pltpu.VMEM((8, 8, 128), F32),
            pltpu.VMEM((4, 8, block), F32),
            dma((3, 4, 2)),
            dma((3, 4)),
            dma((3, 2)),
            dma((3, 4)),
            dma((3,)),
            dma((3,)),
            dma((4,)),
            dma((4,)),
            dma((4, 4)),
            dma((4, 4)),
            dma((4,)),
            dma((4,)),
            dma((8,)),
            dma((8,)),
            dma((4, 3)),
            dma((4, 4)),
            dma((3,)),
            dma((4,)),
            dma((4,)),
            dma((4,)),
            dma((4,)),
            dma((4,)),
        ],
        compiler_params=pltpu.CompilerParams(
            collective_id=0, has_side_effects=True, vmem_limit_bytes=56 * 1024 * 1024
        ),
        name="distill",
    )(teacher_in, teacher_weight, student_in, projection, owner_order.reshape(1, block))
    return grad_matmul(st, dz), cos.reshape(block)


def shards(teacher_in, teacher_weight, student_in, projection, owner_order):
    teacher_all = lax.all_gather(teacher_in, "dp", axis=0, tiled=True)
    student_all = lax.all_gather(student_in, "dp", axis=0, tiled=True)
    groups = lax.axis_size("mp")
    total_rows = teacher_all.shape[0]
    block_len = total_rows // groups
    sub_len = block_len // groups
    slab = teacher_all
    owned = lax.psum_scatter(
        jnp.dot(slab, teacher_weight, preferred_element_type=jnp.float32).astype(jnp.bfloat16),
        "mp",
        scatter_dimension=0,
        tiled=True,
    )
    picked = owned[owner_order].reshape(groups, sub_len, owned.shape[1])
    arrived = lax.all_to_all(picked, "mp", split_axis=0, concat_axis=0, tiled=True)
    target = arrived.reshape(block_len, owned.shape[1])
    slab = student_all
    student_out = lax.psum_scatter(
        jnp.dot(slab, projection, preferred_element_type=jnp.float32).astype(jnp.bfloat16),
        "mp",
        scatter_dimension=0,
        tiled=True,
    ).astype(jnp.float32)
    target_f = target.astype(jnp.float32)
    inner, sq_student, sq_target = lax.psum(
        (
            jnp.sum(student_out * target_f, axis=1),
            jnp.sum(student_out * student_out, axis=1),
            jnp.sum(target_f * target_f, axis=1),
        ),
        "dp",
    )
    inv_student = lax.rsqrt(sq_student + 1e-06)
    inv_target = lax.rsqrt(sq_target + 1e-06)
    cosine = inner * inv_student * inv_target
    scale = -1.0 / total_rows
    grad_out = scale * (
        target_f * (inv_student * inv_target)[:, None]
        - (inner * inv_target * inv_student**3)[:, None] * student_out
    )
    grad_out = grad_out.astype(jnp.bfloat16)
    projection_grad = lax.dot_general(
        student_all,
        lax.all_gather(grad_out, "mp", axis=0, tiled=True),
        (((0,), (0,)), ((), ())),
        preferred_element_type=jnp.float32,
    )
    return (projection_grad, cosine)


def solution(mesh):
    fits = mesh.shape["dp"] == 8 and mesh.shape["mp"] == 4

    def step(teacher_in, teacher_weight, student_in, projection, owner_order):
        args = (teacher_in, teacher_weight, student_in, projection, owner_order)
        if fits:
            return fused_shards(owner_order.shape[0] * mesh.shape["mp"], *args)
        return shards(*args)

    return jax.shard_map(
        step,
        mesh=mesh,
        in_specs=(P("dp", "mp"), P("mp", "dp"), P("dp", "mp"), P("mp", "dp"), P("mp")),
        out_specs=(P("mp", "dp"), P("mp")),
        check_vma=False,
    )
```

```python
import functools

import jax
import jax.numpy as jnp
from jax import lax
from jax.experimental import pallas as pl
from jax.experimental.pallas import tpu as pltpu
from jax.sharding import PartitionSpec as P

MESH = pl.DeviceIdType.MESH
F32 = jnp.float32
BF16 = jnp.bfloat16
TILE = 256


def kernel(
    total_rows,
    teacher_ref, weight_ref, student_ref, projection_ref, order_ref,
    cos_ref, dz_ref, st_ref,
    xbuf, wbuf, acc, stv, obuf, tsend, trecv, ssend, srecv, tall, zall, dzv, stm, statr, coef,
    x_recv, send_a, send_b, send_x, local_x, local_w, o_send, o_recv,
    t_send, t_recv, s_send, s_recv, q_send, q_recv, g_send, g_recv, z_send, z_recv, c_send, c_recv,
    local_st, local_dz,
):
    dp, mp = lax.axis_index("dp"), lax.axis_index("mp")
    z, x = dp // 2, dp % 2
    ox = 1 - x
    za = z + 1 - 2 * (z % 2)
    zb = 3 - z
    half = z // 2
    mid = (z + 1) // 2 == 1
    order = [z, za, 2 - half, 3 - 3 * half]
    rows, width = xbuf.shape[3], xbuf.shape[4]
    block = 2 * rows
    sub = tsend.shape[2]
    cols = wbuf.shape[2]
    tiles = cols // TILE
    groups = 4

    def at(plane, column):
        return (2 * plane + column, mp)

    def mpd(other):
        return (dp, other)

    def other_mp(d):
        return (mp + d) % groups

    def own_src(t):
        if t > 0:
            return teacher_ref.at[:, pl.ds((t - 1) * width, width)]
        return student_ref

    w_copies = []
    x_copies = []
    for t in range(3):
        x_copies.append(pltpu.make_async_copy(own_src(t), xbuf.at[t, z, x], local_x.at[t]))
        src = weight_ref.at[pl.ds((t - 1) * width, width), :] if t > 0 else projection_ref
        w_copies.append(pltpu.make_async_copy(src, wbuf.at[t], local_w.at[t]))
    for t in range(3):
        x_copies[t].start()
        w_copies[t].start()

    barrier = pltpu.get_barrier_semaphore()
    for d in range(1, 8):
        pl.semaphore_signal(barrier, inc=1, device_id=((dp + d) % 8, mp), device_id_type=MESH)
    for d in range(1, groups):
        pl.semaphore_signal(barrier, inc=1, device_id=mpd(other_mp(d)), device_id_type=MESH)
    pl.semaphore_wait(barrier, 7 + groups - 1)

    def remote(src, dst, ssem, rsem, device):
        return pltpu.make_async_remote_copy(
            src_ref=src, dst_ref=dst, send_sem=ssem, recv_sem=rsem,
            device_id=device, device_id_type=MESH,
        )

    def copy_x(t, i):
        src = own_src(t) if i == 0 else xbuf.at[t, order[i], x]
        return remote(src, xbuf.at[t, order[i], x], send_x.at[t, i], x_recv.at[t, order[i], x], at(z, ox))

    def copy_a(t, i):
        if i == 1:
            src, s, c = xbuf.at[t, z, ox], z, ox
        else:
            s, c = order[i], x
            src = own_src(t) if i == 0 else xbuf.at[t, s, c]
        return remote(src, xbuf.at[t, s, c], send_a.at[t, i], x_recv.at[t, s, c], at(za, x))

    def copy_b(t, i):
        s = order[i]
        src = own_src(t) if i == 0 else xbuf.at[t, s, x]
        return remote(src, xbuf.at[t, s, x], send_b.at[t, i], x_recv.at[t, s, x], at(zb, x))

    def wait_piece(t, s, c):
        pltpu.make_async_copy(xbuf.at[t, s, c], xbuf.at[t, s, c], x_recv.at[t, s, c]).wait()

    def start_on(middle, *copies):
        @pl.when(mid if middle else jnp.logical_not(mid))
        def _():
            for c in copies:
                c.start()

    def event(t, i, middle):
        @pl.when(mid if middle else jnp.logical_not(mid))
        def _():
            wait_piece(t, order[i], x)
            if middle:
                (copy_b(t, 1) if i == 1 else copy_a(t, i)).start()
            if not (t == 2 and i == 1):
                copy_x(t, i).start()

    def other(t, i):
        wait_piece(t, order[i], ox)

    def dot_block(t, b, cs):
        return jnp.dot(xbuf[t, b].reshape(block, width), wbuf[t, :, cs], preferred_element_type=F32)

    def tile_loop(body):
        def step(j, carry):
            body(pl.ds(pl.multiple_of(j * TILE, TILE), TILE))
            return carry

        lax.fori_loop(0, tiles, step, 0)

    def spread(b):
        hit = lax.broadcasted_iota(jnp.int32, (block, block), 0) == jnp.broadcast_to(obuf[b], (block, block))
        return jnp.where(hit, 1.0, 0.0).astype(BF16)

    def permute(b, part, cs):
        picked = lax.dot_general(spread(b), part, (((0,), (0,)), ((), ())), preferred_element_type=F32)
        tsend[b, :, :, cs] = picked.astype(BF16).reshape(groups, sub, TILE)

    def teacher_send(i):
        b = order[i]
        for d in range(1, groups):
            o = other_mp(d)
            remote(tsend.at[b, o], trecv.at[mp, b], t_send.at[i, d], t_recv.at[mp, b], mpd(o)).start()

    def teacher_first(i):
        b = order[i]

        def body(cs):
            acc[b, :, cs] = dot_block(1, b, cs)

        tile_loop(body)

    def teacher_second(i):
        b = order[i]

        def body(cs):
            permute(b, (acc[b, :, cs] + dot_block(2, b, cs)).astype(BF16), cs)

        tile_loop(body)
        teacher_send(i)

    def student_copy(b):
        return remote(ssend.at[b], srecv.at[mp], s_send.at[b], s_recv.at[mp], mpd(b))

    def student(i):
        b = order[i]

        def body(cs):
            ssend[b, :, cs] = dot_block(0, b, cs).astype(BF16)

        tile_loop(body)

        @pl.when(mp != b)
        def _():
            student_copy(b).start()

    def st_copy(i):
        b = order[i]
        return pltpu.make_async_copy(
            stv.at[b], st_ref.at[:, pl.ds(pl.multiple_of(b * block, block), block)], local_st.at[i]
        )

    def transpose(i):
        b = order[i]

        def step(j, carry):
            ks = pl.ds(pl.multiple_of(j * TILE, TILE), TILE)
            stv[b, ks, :] = xbuf[0, b, :, :, ks].reshape(block, TILE).T
            return carry

        lax.fori_loop(0, width // TILE, step, 0)
        st_copy(i).start()

    obuf[mp] = order_ref[...]
    o_copies = [
        remote(order_ref, obuf.at[mp], o_send.at[d], o_recv.at[mp], mpd(other_mp(d))) for d in range(1, groups)
    ]

    CH = 16
    core = mp + 1 - 2 * (mp % 2)
    across = (mp + 2) % 4
    across_core = (core + 2) % 4

    def arrived(ref, sem):
        pltpu.make_async_copy(ref, ref, sem).wait()

    def z_copy(k):
        o, to = ((mp, across), (mp, core), (across, core))[k]
        return remote(zall.at[o], zall.at[o], z_send.at[k], z_recv.at[o], mpd(to))

    def student_sum():
        for d in range(1, groups):
            o = other_mp(d)
            arrived(srecv.at[o], s_recv.at[o])

        def step(r, carry):
            rs = pl.ds(pl.multiple_of(r * CH, CH), CH)
            total = ssend[mp, rs, :].astype(F32)
            for d in range(1, groups):
                total = total + srecv[other_mp(d), rs, :].astype(F32)
            zall[mp, rs, :] = total
            return carry

        lax.fori_loop(0, block // CH, step, 0)
        z_copy(0).start()
        z_copy(1).start()

    def student_relay():
        arrived(zall.at[across], z_recv.at[across])
        z_copy(2).start()

    def g_copy(i, k):
        b = order[i]
        o, to = ((mp, across), (mp, core), (across, core))[k]
        return remote(tall.at[o, b], tall.at[o, b], g_send.at[i, k], g_recv.at[o, b], mpd(to))

    def target_sum(i):
        b = order[i]
        for d in range(1, groups):
            o = other_mp(d)
            arrived(trecv.at[o, b], t_recv.at[o, b])
        for r in range(sub // CH):
            rs = pl.ds(r * CH, CH)
            total = tsend[b, mp, rs, :].astype(F32)
            for d in range(1, groups):
                total = total + trecv[other_mp(d), b, rs, :].astype(F32)
            tall[mp, b, rs, :] = total.astype(BF16)
        g_copy(i, 0).start()
        g_copy(i, 1).start()
        for r in range(sub // CH):
            rows_here = pl.ds(pl.multiple_of(b * sub + r * CH, CH), CH)
            tt = tall[mp, b, pl.ds(r * CH, CH), :].astype(F32)
            zz = zall[mp, rows_here, :]
            lane = lax.broadcasted_iota(jnp.int32, (CH, 128), 1)
            s0 = jnp.sum(zz * tt, axis=1, keepdims=True)
            s1 = jnp.sum(zz * zz, axis=1, keepdims=True)
            s2 = jnp.sum(tt * tt, axis=1, keepdims=True)
            stm[rows_here, :] = jnp.where(lane == 0, s0, jnp.where(lane == 1, s1, jnp.where(lane == 2, s2, 0.0)))

    def target_relay(i):
        b = order[i]
        arrived(tall.at[across, b], g_recv.at[across, b])
        g_copy(i, 2).start()

    for t in range(2):
        copy_a(t, 0).start()
        start_on(True, copy_b(t, 0))
        copy_x(t, 0).start()
    for c in o_copies:
        c.start()
    event(0, 1, True)
    event(1, 1, True)
    event(0, 2, True)
    event(1, 2, True)
    start_on(True, copy_b(2, 0), copy_x(2, 0))
    event(0, 1, False)
    x_copies[0].wait()
    w_copies[0].wait()
    other(0, 0)
    student(0)
    event(1, 1, False)
    start_on(False, copy_a(2, 0))
    x_copies[1].wait()
    w_copies[1].wait()
    event(0, 3, True)
    other(1, 0)
    teacher_first(0)
    event(0, 2, False)
    event(1, 3, True)
    start_on(True, copy_a(2, 0))
    other(0, 1)
    student(1)
    event(1, 2, False)
    start_on(False, copy_x(2, 0))
    event(2, 1, True)
    other(1, 1)
    teacher_first(1)
    event(0, 3, False)
    event(2, 2, True)
    other(0, 2)
    student(2)
    event(1, 3, False)
    other(1, 2)
    teacher_first(2)
    event(2, 3, True)
    x_copies[2].wait()
    w_copies[2].wait()
    for d in range(1, groups):
        o = other_mp(d)
        arrived(obuf.at[o], o_recv.at[o])
    other(2, 0)
    copy_a(2, 1).start()
    teacher_second(0)
    event(2, 2, False)
    other(0, 3)
    student(3)
    event(2, 3, False)
    other(1, 3)
    teacher_first(3)
    student_sum()
    transpose(0)
    transpose(1)

    @pl.when(jnp.logical_not(mid))
    def _():
        wait_piece(2, order[1], x)

    other(2, 1)
    teacher_second(1)
    target_sum(0)
    other(2, 2)
    teacher_second(2)
    target_sum(1)
    target_relay(0)
    student_relay()
    other(2, 3)
    teacher_second(3)
    target_sum(2)
    target_relay(1)
    target_sum(3)

    statr[dp] = stm[...].T[0:8, :]
    q_copies = []
    for d in range(1, 8):
        o = (dp + d) % 8
        q_copies.append(remote(statr.at[dp], statr.at[dp], q_send.at[d], q_recv.at[dp], (o, mp)))
    for c in q_copies:
        c.start()
    target_relay(2)
    transpose(2)
    target_relay(3)
    transpose(3)
    for d in range(1, 8):
        o = (dp + d) % 8
        arrived(statr.at[o], q_recv.at[o])
    sums = statr[0]
    for s in range(1, 8):
        sums = sums + statr[s]
    inner = sums[0:1, :]
    inv_s = lax.rsqrt(sums[1:2, :] + 1e-06)
    inv_t = lax.rsqrt(sums[2:3, :] + 1e-06)
    cos_ref[...] = inner * inv_s * inv_t
    scale = -1.0 / total_rows
    on_target = jnp.broadcast_to(scale * (inv_s * inv_t), (8, block))
    on_student = jnp.broadcast_to(scale * (inner * inv_t * inv_s * inv_s * inv_s), (8, block))
    row = lax.broadcasted_iota(jnp.int32, (8, block), 0)
    coef[mp] = jnp.where(row == 0, on_target, jnp.where(row == 1, on_student, 0.0))
    c_copies = [
        remote(coef.at[mp], coef.at[mp], c_send.at[d], c_recv.at[mp], mpd(other_mp(d))) for d in range(1, groups)
    ]
    for c in c_copies:
        c.start()

    def dz_copy(k, o):
        here = pl.ds(pl.multiple_of(o * block, block), block)
        return pltpu.make_async_copy(dzv.at[o], dz_ref.at[here, :], local_dz.at[k])

    owners = (mp, core, across, across_core)
    for k, o in enumerate(owners):
        if k > 0:
            arrived(coef.at[o], c_recv.at[o])
            if k != 2:
                for b in range(4):
                    arrived(tall.at[o, b], g_recv.at[o, b])
                arrived(zall.at[o], z_recv.at[o])
        stm[...] = jnp.concatenate([coef[o], jnp.zeros((block - 8, block), F32)], axis=0).T

        def dz_step(r, carry):
            rs = pl.ds(pl.multiple_of(r * CH, CH), CH)
            b, part = r * CH // sub, pl.ds(pl.multiple_of(r * CH % sub, CH), CH)
            both = stm[rs, :]
            dzv[o, rs, :] = (tall[o, b, part, :].astype(F32) * both[:, 0:1] - zall[o, rs, :] * both[:, 1:2]).astype(BF16)
            return carry

        lax.fori_loop(0, block // CH, dz_step, 0)
        dz_copy(k, o).start()

    for c in c_copies + q_copies + o_copies + [z_copy(k) for k in range(3)]:
        c.wait_send()
    for t in range(3):
        copy_a(t, 0).wait_send()
        for i in range(groups):
            if not (t == 2 and i == 1):
                copy_x(t, i).wait_send()

        @pl.when(mid)
        def _():
            copy_b(t, 0).wait_send()
            copy_b(t, 1).wait_send()
            copy_a(t, 2).wait_send()
            copy_a(t, 3).wait_send()

    copy_a(2, 1).wait_send()
    for i in range(groups):
        b = order[i]
        for d in range(1, groups):
            o = other_mp(d)
            remote(tsend.at[b, o], trecv.at[mp, b], t_send.at[i, d], t_recv.at[mp, b], mpd(o)).wait_send()
        for k in range(3):
            g_copy(i, k).wait_send()

        @pl.when(mp != b)
        def _():
            student_copy(b).wait_send()

        st_copy(i).wait()
        dz_copy(i, owners[i]).wait()


def grad_kernel(st_ref, dz_ref, out_ref, st, dz, out, load, dz_load, store):
    steps = st.shape[0]

    def rows(j):
        return pl.ds(pl.multiple_of(j * TILE, TILE), TILE)

    def fetch(j):
        return pltpu.make_async_copy(st_ref.at[rows(j), :], st.at[j], load.at[j])

    def put(j):
        return pltpu.make_async_copy(out.at[j], out_ref.at[rows(j), :], store.at[j])

    whole = pltpu.make_async_copy(dz_ref, dz, dz_load)
    whole.start()
    for j in range(steps):
        fetch(j).start()
    whole.wait()

    def step(j, carry):
        fetch(j).wait()
        out[j] = jnp.dot(st[j], dz[...], preferred_element_type=F32)
        put(j).start()
        return carry

    lax.fori_loop(0, steps, step, 0)
    for j in range(steps):
        put(j).wait()


def grad_matmul(st, dz):
    width, depth = st.shape
    cols = dz.shape[1]
    steps = width // TILE
    any_spec = pl.BlockSpec(memory_space=pl.ANY)
    dma = pltpu.SemaphoreType.DMA
    return pl.pallas_call(
        grad_kernel,
        in_specs=[any_spec, any_spec],
        out_specs=any_spec,
        out_shape=jax.ShapeDtypeStruct((width, cols), F32),
        scratch_shapes=[
            pltpu.VMEM((steps, TILE, depth), BF16),
            pltpu.VMEM((depth, cols), BF16),
            pltpu.VMEM((steps, TILE, cols), F32),
            dma((steps,)),
            dma(()),
            dma((steps,)),
        ],
        compiler_params=pltpu.CompilerParams(vmem_limit_bytes=56 * 1024 * 1024),
        name="grad",
    )(st, dz)


def fused_shards(total_rows, teacher_in, teacher_weight, student_in, projection, owner_order):
    rows, width = student_in.shape
    cols = projection.shape[1]
    block = owner_order.shape[0]
    groups = total_rows // block
    sub = block // groups
    any_spec = pl.BlockSpec(memory_space=pl.ANY)
    vmem_spec = pl.BlockSpec(memory_space=pltpu.VMEM)
    dma = pltpu.SemaphoreType.DMA
    cos, dz, st = pl.pallas_call(
        functools.partial(kernel, total_rows),
        out_shape=(
            jax.ShapeDtypeStruct((1, block), F32),
            jax.ShapeDtypeStruct((total_rows, cols), BF16),
            jax.ShapeDtypeStruct((width, total_rows), BF16),
        ),
        in_specs=[any_spec] * 4 + [vmem_spec],
        out_specs=(vmem_spec, any_spec, any_spec),
        scratch_shapes=[
            pltpu.VMEM((3, 4, 2, rows, width), BF16),
            pltpu.VMEM((3, width, cols), BF16),
            pltpu.VMEM((4, block, cols), F32),
            pltpu.VMEM((4, width, block), BF16),
            pltpu.VMEM((4, 1, block), jnp.int32),
            pltpu.VMEM((4, groups, sub, cols), BF16),
            pltpu.VMEM((4, groups, sub, cols), BF16),
            pltpu.VMEM((4, block, cols), BF16),
            pltpu.VMEM((4, block, cols), BF16),
            pltpu.VMEM((4, groups, sub, cols), BF16),
            pltpu.VMEM((4, block, cols), F32),
            pltpu.VMEM((4, block, cols), BF16),
            pltpu.VMEM((block, 128), F32),
            pltpu.VMEM((8, 8, 128), F32),
            pltpu.VMEM((4, 8, block), F32),
            dma((3, 4, 2)),
            dma((3, 4)),
            dma((3, 2)),
            dma((3, 4)),
            dma((3,)),
            dma((3,)),
            dma((4,)),
            dma((4,)),
            dma((4, 4)),
            dma((4, 4)),
            dma((4,)),
            dma((4,)),
            dma((8,)),
            dma((8,)),
            dma((4, 3)),
            dma((4, 4)),
            dma((3,)),
            dma((4,)),
            dma((4,)),
            dma((4,)),
            dma((4,)),
            dma((4,)),
        ],
        compiler_params=pltpu.CompilerParams(
            collective_id=0, has_side_effects=True, vmem_limit_bytes=56 * 1024 * 1024
        ),
        name="distill",
    )(teacher_in, teacher_weight, student_in, projection, owner_order.reshape(1, block))
    return grad_matmul(st, dz), cos.reshape(block)


def shards(teacher_in, teacher_weight, student_in, projection, owner_order):
    teacher_all = lax.all_gather(teacher_in, "dp", axis=0, tiled=True)
    student_all = lax.all_gather(student_in, "dp", axis=0, tiled=True)
    groups = lax.axis_size("mp")
    total_rows = teacher_all.shape[0]
    block_len = total_rows // groups
    sub_len = block_len // groups
    slab = teacher_all
    owned = lax.psum_scatter(
        jnp.dot(slab, teacher_weight, preferred_element_type=jnp.float32).astype(jnp.bfloat16),
        "mp",
        scatter_dimension=0,
        tiled=True,
    )
    picked = owned[owner_order].reshape(groups, sub_len, owned.shape[1])
    arrived = lax.all_to_all(picked, "mp", split_axis=0, concat_axis=0, tiled=True)
    target = arrived.reshape(block_len, owned.shape[1])
    slab = student_all
    student_out = lax.psum_scatter(
        jnp.dot(slab, projection, preferred_element_type=jnp.float32).astype(jnp.bfloat16),
        "mp",
        scatter_dimension=0,
        tiled=True,
    ).astype(jnp.float32)
    target_f = target.astype(jnp.float32)
    inner, sq_student, sq_target = lax.psum(
        (
            jnp.sum(student_out * target_f, axis=1),
            jnp.sum(student_out * student_out, axis=1),
            jnp.sum(target_f * target_f, axis=1),
        ),
        "dp",
    )
    inv_student = lax.rsqrt(sq_student + 1e-06)
    inv_target = lax.rsqrt(sq_target + 1e-06)
    cosine = inner * inv_student * inv_target
    scale = -1.0 / total_rows
    grad_out = scale * (
        target_f * (inv_student * inv_target)[:, None]
        - (inner * inv_target * inv_student**3)[:, None] * student_out
    )
    grad_out = grad_out.astype(jnp.bfloat16)
    projection_grad = lax.dot_general(
        student_all,
        lax.all_gather(grad_out, "mp", axis=0, tiled=True),
        (((0,), (0,)), ((), ())),
        preferred_element_type=jnp.float32,
    )
    return (projection_grad, cosine)


def solution(mesh):
    fits = mesh.shape["dp"] == 8 and mesh.shape["mp"] == 4

    def step(teacher_in, teacher_weight, student_in, projection, owner_order):
        args = (teacher_in, teacher_weight, student_in, projection, owner_order)
        if fits:
            return fused_shards(owner_order.shape[0] * mesh.shape["mp"], *args)
        return shards(*args)

    return jax.shard_map(
        step,
        mesh=mesh,
        in_specs=(P("dp", "mp"), P("mp", "dp"), P("dp", "mp"), P("mp", "dp"), P("mp")),
        out_specs=(P("mp", "dp"), P("mp")),
        check_vma=False,
    )
```
